256 devices in a mesh: ctx: 32 (over z, x), head: 8 (over y, core).
Axes of the slice: x: 4, y: 4, z: 8, core: 2. Of those that a mesh axis runs over, the one named last changes fastest.
Arguments:
- activations: bfloat16 [32768, 2048], P('ctx'), may hold values from -6 to 6
- qkv_weight: bfloat16 [2048, 6144], P(None, 'head'), may hold values from -0.125 to 0.125
- level_proj: bfloat16 [2048, 336], P(None, 'head'), may hold values from -0.125 to 0.125
- log_gate: float32 [32768, 16], P('ctx', 'head'), may hold values from -4 to 0, as said below
- prior_parts: float32 [32, 4, 16, 128, 128], P('ctx', None, 'head'), may hold values from -18 to 18
- out_weight: bfloat16 [2048, 2048], P('head'), may hold values from -0.125 to 0.125
Outputs:
- layer_out: bfloat16 [32768, 2048], P(('ctx', 'head'))
The draws below stay inside these ranges and needn't reach their ends.
Inputs may be any that keep to these rules, and one draw needn't show every extreme that they name: `log_gate`: every entry is negative.
All inputs are finite; a program needn't handle non-finite values.
Results may differ from the reference program's by a relative error of at most 0.023.
Values may be sent and summed in bfloat16 or wider, within the bound.
No kernel may reach another device: no remote copies, remote signals or barrier semaphores. Data moves between devices by JAX's collectives and lax.ppermute only.
A program may use at most 128 MiB of HBM per device.

```python
import math
import jax
import jax.numpy as jnp
from jax import lax

D = 2048
HEAD_COUNT = 16
DH = 128
LEVELS = 21
PRIOR = 4
TOK_CTX = 1024
WINDOW_TOKENS = 32768
N_CTX = 32


def draw_log_gate(key, part):
    key = jax.random.fold_in(key, 11)
    random_subkeys = jax.random.split(key, 7)
    blocks = WINDOW_TOKENS // TOK_CTX
    fast_tenths = 5
    spread = 0.5
    fast_heads = jax.random.randint(random_subkeys[0], (HEAD_COUNT,), 0, 10) < fast_tenths
    fast_len = jnp.minimum(jax.random.uniform(random_subkeys[1], (HEAD_COUNT,), jnp.float32, 30.0, 50.0), TOK_CTX / 4.0)
    slow_rate = jnp.exp(jax.random.uniform(random_subkeys[2], (HEAD_COUNT,), jnp.float32, math.log(0.3), math.log(0.7))) / WINDOW_TOKENS
    head_decay_rate = jnp.where(fast_heads, 3.0 / fast_len, slow_rate)
    block_tokens = jnp.exp(jax.random.uniform(random_subkeys[3], (blocks, HEAD_COUNT), jnp.float32, math.log(0.5), math.log(2.0)))
    block_tokens = jnp.repeat(block_tokens, TOK_CTX, axis=0)
    jitter_amount = jax.random.uniform(random_subkeys[4], (WINDOW_TOKENS, HEAD_COUNT), jnp.float32, 1.0 - spread, 1.0 + spread)
    spike_mask = jax.random.randint(random_subkeys[5], (WINDOW_TOKENS, HEAD_COUNT), 0, WINDOW_TOKENS) < 3
    spike_logarithm = jnp.log(jax.random.uniform(random_subkeys[6], (WINDOW_TOKENS, HEAD_COUNT), jnp.float32, 0.5, 0.8))
    return -head_decay_rate[None] * block_tokens * jitter_amount + jnp.where(spike_mask, spike_logarithm, 0.0)


def levels(rng, shape, pieces, smallest, high):
    def one(position, shards_of):
        steps = jax.random.uniform(jax.random.fold_in(jax.random.fold_in(rng, 6), position), (shards_of,), jnp.float32, smallest / len(pieces), high / len(pieces))
        return jnp.repeat(jnp.exp(steps), shape[position] // shards_of).reshape((-1,) + (1,) * (len(shape) - position - 1))

    loudness = one(*pieces[0])
    for cut in pieces[1:]:
        loudness = loudness * one(*cut)
    return loudness


def normal_values(own_key, shape, width, most, pieces=(), kind=jnp.bfloat16):
    array = width * jax.random.normal(own_key, shape, jnp.float32)
    if pieces:
        array = array * levels(own_key, shape, pieces, -0.22, 0.18)
    return jnp.clip(array, -most, most).astype(kind)


def setup_inputs(seed: int = 0) -> dict:
    splits = jax.random.split(jax.random.key(seed), 7)
    return {
        "activations": normal_values(splits[0], (WINDOW_TOKENS, D), 1.0, 6.0, ((0, 32),)),
        "qkv_weight": normal_values(splits[1], (D, 3 * HEAD_COUNT * DH), D ** -0.5, 0.125, ((1, 8),)),
        "level_proj": normal_values(splits[2], (D, HEAD_COUNT * LEVELS), D ** -0.5, 0.125, ((1, 8),)),
        "log_gate": draw_log_gate(jax.random.fold_in(splits[6], 71), 0),
        "prior_parts": normal_values(splits[4], (N_CTX, PRIOR, HEAD_COUNT, DH, DH), 3.0, 18.0, ((0, 32), (2, 8)), jnp.float32),
        "out_weight": normal_values(splits[5], (HEAD_COUNT * DH, D), (HEAD_COUNT * DH) ** -0.5, 0.125, ((0, 8),)),
    }


def level_of(left, right):
    differing = jnp.bitwise_xor(left, right)
    counted = jnp.zeros_like(differing)
    for bit_number in range(31):
        counted = counted + (jnp.right_shift(differing, bit_number) > 0).astype(jnp.int32)
    return counted

def reference(activations, qkv_weight, level_proj, log_gate, prior_parts, out_weight):
    blocks = N_CTX
    block_len = WINDOW_TOKENS // N_CTX
    ctx_bits = blocks.bit_length() - 1
    base_level = block_len.bit_length()
    prior_level = WINDOW_TOKENS.bit_length()
    query_scale = DH ** (-0.5)
    highest = lax.Precision.HIGHEST
    projected = jnp.dot(activations, qkv_weight, preferred_element_type=jnp.float32).astype(jnp.bfloat16)
    projected = projected.reshape(blocks, block_len, HEAD_COUNT, 3, DH)
    queries = projected[:, :, :, 0].astype(jnp.float32)
    key_rows = projected[:, :, :, 1].astype(jnp.float32)
    values = projected[:, :, :, 2].astype(jnp.float32)
    level_weight = jax.nn.softplus(jnp.dot(activations, level_proj, preferred_element_type=jnp.float32))
    level_weight = level_weight.reshape(blocks, block_len, HEAD_COUNT, LEVELS)
    cumulative = jnp.cumsum(log_gate, axis=0).reshape(blocks, block_len, HEAD_COUNT)
    block_end = cumulative[:, -1]
    summaries = jnp.einsum('bsh,bshi,bshj->bhij', jnp.exp(block_end[:, None] - cumulative), key_rows, values, precision=highest)
    earlier = lax.optimization_barrier(jnp.sum(prior_parts, axis=0))
    positions = jnp.arange(block_len, dtype=jnp.int32)
    local_levels = level_of(positions[:, None], positions[None, :])
    causal = positions[:, None] >= positions[None, :]
    block_ids = jnp.arange(blocks, dtype=jnp.int32)
    bit_index = jnp.arange(ctx_bits, dtype=jnp.int32)

    def one_block(block_index):
        query_block = queries[block_index]
        key_block = key_rows[block_index]
        value_block = values[block_index]
        cum_block = cumulative[block_index]
        level_block = level_weight[block_index]
        scores = jnp.einsum('thd,shd->hts', query_block, key_block, precision=highest) * query_scale
        cum_heads = jnp.transpose(cum_block)
        gap_matrix = cum_heads[:, :, None] - cum_heads[:, None, :]
        decay_matrix = jnp.where(causal[None], jnp.exp(jnp.where(causal[None], gap_matrix, 0.0)), 0.0)
        weight_heads = jnp.transpose(level_block, (1, 0, 2))
        pair_index = jnp.broadcast_to(local_levels[None], (HEAD_COUNT, block_len, block_len))
        pair_weight = jnp.take_along_axis(weight_heads, pair_index, axis=2)
        mixing = (pair_weight * decay_matrix * scores).astype(jnp.bfloat16)
        inside = jnp.einsum('hts,shj->thj', mixing.astype(jnp.float32), value_block, precision=highest)
        prev_end = jnp.where(block_index > 0, block_end[jnp.maximum(block_index - 1, 0)], 0.0)
        same_high = jnp.right_shift(block_ids[None], bit_index[:, None] + 1) == jnp.right_shift(block_index, bit_index + 1)[:, None]
        bit_zero = jnp.bitwise_and(jnp.right_shift(block_ids[None], bit_index[:, None]), 1) == 0
        bit_one = jnp.bitwise_and(jnp.right_shift(block_index, bit_index), 1) == 1
        group_mask = (same_high & bit_zero & bit_one[:, None]).astype(jnp.float32)
        valid_rows = block_ids < block_index
        decay_gap = jnp.where(valid_rows[:, None], prev_end[None] - block_end, 0.0)
        carry_factor = jnp.where(valid_rows[:, None], jnp.exp(decay_gap), 0.0)
        coefficient = group_mask[:, :, None] * carry_factor[None]
        states = jnp.einsum('kjh,jhab->khab', coefficient, summaries, precision=highest)
        stacked = jnp.concatenate([states, earlier], axis=0).astype(jnp.bfloat16).astype(jnp.float32)
        reads = jnp.einsum('thi,nhij->tnhj', query_block, stacked, precision=highest)
        across_weight = level_block[:, :, base_level:base_level + ctx_bits] * jnp.exp(cum_block - prev_end[None])[:, :, None] * query_scale
        across = lax.optimization_barrier(jnp.sum(jnp.transpose(across_weight, (0, 2, 1))[:, :, :, None] * reads[:, :ctx_bits], axis=1))
        prior_weight = level_block[:, :, prior_level:prior_level + PRIOR] * jnp.exp(cum_block)[:, :, None] * query_scale
        prior_term = lax.optimization_barrier(jnp.sum(jnp.transpose(prior_weight, (0, 2, 1))[:, :, :, None] * reads[:, ctx_bits:], axis=1))
        mixed_heads = inside + across + prior_term
        normed = mixed_heads * lax.rsqrt(lax.optimization_barrier(jnp.mean(mixed_heads * mixed_heads, axis=-1, keepdims=True)) + 1e-06)
        return normed.astype(jnp.bfloat16).reshape(block_len, HEAD_COUNT * DH)
    normed_all = lax.map(one_block, block_ids).reshape(WINDOW_TOKENS, HEAD_COUNT * DH)
    return jnp.dot(normed_all, out_weight, preferred_element_type=jnp.float32).astype(jnp.bfloat16)
```

```python
import functools

import jax
import jax.numpy as jnp
from jax import lax
from jax.experimental import pallas as pl
from jax.experimental.pallas import tpu as pltpu
from jax.sharding import PartitionSpec as P

DH = 128
LEVELS = 21
PRIOR = 4
CHUNK = 128
TILE = 256
NX = 4
TAIL = 16
VMEM = pl.BlockSpec(memory_space=pltpu.VMEM)
SMEM = pl.BlockSpec(memory_space=pltpu.SMEM)
F32 = jnp.float32
BF16 = jnp.bfloat16


def params(mib=48):
    return pltpu.CompilerParams(vmem_limit_bytes=mib * 1024 * 1024)


def dot(left, right, contract=((1,), (0,))):
    return lax.dot_general(left, right, (contract, ((), ())), preferred_element_type=F32)


def iota(axis, shape=(CHUNK, CHUNK)):
    return lax.broadcasted_iota(jnp.int32, shape, axis)


def decay_rows(decays):
    rows = iota(0, (TAIL, DH))
    tail = jnp.zeros((TAIL, DH), F32)
    for index, decay in enumerate(decays):
        rest = jnp.broadcast_to(decay, (1, DH))
        for piece in range(3):
            part = rest.astype(BF16).astype(F32)
            tail = jnp.where(rows == index * 3 + piece, part, tail)
            rest = rest - part
    return tail.astype(BF16)


def tail_decays(tail, heads):
    tail = tail.astype(F32)
    return [
        (tail[3 * h : 3 * h + 1] + tail[3 * h + 1 : 3 * h + 2]) + tail[3 * h + 2 : 3 * h + 3]
        for h in range(heads)
    ]


def decays_of(payload, heads):
    return tail_decays(payload[heads * DH : heads * DH + TAIL, :], heads)


def copy_parts(source, target, sems):
    count = sems.shape[0]
    size = target.shape[0] // count
    copies = []
    for i in range(count):
        part = pl.ds(i * size, size)
        copies.append(pltpu.make_async_copy(source.at[part, :], target.at[part, :], sems.at[i]))
        copies[-1].start()
    return copies


def keys_kernel(acts_hbm, weight_hbm, kv, query_weight, acts, weight, weight_sem, acts_sem):
    block = acts.shape[0]
    heads = query_weight.shape[1] // DH
    weight_copies = copy_parts(weight_hbm, weight, weight_sem)
    acts_copies = copy_parts(acts_hbm, acts, acts_sem)
    for copy in weight_copies:
        copy.wait()
    per_tile = len(acts_copies) * TILE // block
    for i in range(block // TILE):
        for copy in acts_copies[i * per_tile : (i + 1) * per_tile]:
            copy.wait()
        token = slice(i * TILE, (i + 1) * TILE)
        for h in range(heads):
            both = dot(acts[token, :], weight[:, h * 3 * DH + DH : (h + 1) * 3 * DH])
            kv[token, h * 2 * DH : (h + 1) * 2 * DH] = both.astype(BF16)
    for h in range(heads):
        query_weight[:, h * DH : (h + 1) * DH] = weight[:, h * 3 * DH : h * 3 * DH + DH]


def states_kernel(place, kv, gate, prior, chunk_states, *payloads):
    x = place[0]
    heads, block = gate.shape
    later = iota(1) > iota(0)
    for h in range(heads):
        rows = slice(h * DH, (h + 1) * DH)
        total = None
        for c in range(block // CHUNK):
            token = slice(c * CHUNK, (c + 1) * CHUNK)
            gates = gate[h : h + 1, token]
            to_end = jnp.exp(jnp.sum(jnp.where(later, gates, 0.0), axis=1, keepdims=True))
            keys = kv[token, 2 * h * DH : (2 * h + 1) * DH].astype(F32)
            values = kv[token, (2 * h + 1) * DH : (2 * h + 2) * DH]
            state = dot((keys * to_end).astype(BF16), values, ((0,), (0,)))
            chunk_states[c, h] = state
            decay = jnp.exp(jnp.sum(gates, axis=1, keepdims=True))
            total = state if total is None else total * decay + state
        for payload in payloads:
            payload[rows, :] = total.astype(BF16)
    tail = decay_rows([jnp.sum(gate[h : h + 1, :], axis=1, keepdims=True) for h in range(heads)])
    start = heads * DH + TAIL
    for d, payload in enumerate(payloads):
        payload[heads * DH : start, :] = tail
        for h in range(heads):
            payload[start + h * DH : start + (h + 1) * DH, :] = prior[x ^ d, h].astype(BF16)


def level_kernel(acts, weight, proj, after, query, level):
    for i in range(acts.shape[0] // TILE):
        rows = slice(i * TILE, (i + 1) * TILE)
        query[rows, :] = dot(acts[rows, :], weight[...]).astype(BF16)
        raw = dot(acts[rows, :], proj[...], ((1,), (1,)))
        value = (jnp.maximum(raw, 0.0) + jnp.log1p(jnp.exp(-jnp.abs(raw)))) * DH ** (-0.5)
        pad = jnp.zeros((TILE, DH - value.shape[1]), F32)
        level[rows, :] = jnp.concatenate([value, pad], axis=1)


def attend_kernel(h, query_rows, kv, level, gate, chunk_states, low_states, after, inside):
    chunks = chunk_states.shape[0]
    low_bits = low_states.shape[0]
    rows, columns = iota(0), iota(1)
    causal = rows >= columns
    differing = jnp.bitwise_xor(rows, columns)
    level_index = jnp.full((CHUNK, CHUNK), h * LEVELS, jnp.int32)
    for bit in range(7):
        level_index = level_index + (differing >= (1 << bit)).astype(jnp.int32)

    totals = [
        jnp.sum(gate[h : h + 1, c * CHUNK : (c + 1) * CHUNK], axis=1, keepdims=True)
        for c in range(chunks)
    ]
    states = {}
    sums = [chunk_states[c, h] for c in range(chunks)]
    for bit in range(3):
        width = 1 << bit
        for low in range(0, chunks, 2 * width):
            state = sums[low // width]
            for c in range(low + width, low + 2 * width):
                states[c, bit] = state.astype(BF16)
                state = state * jnp.exp(totals[c])
            sums[low // width] = state + sums[low // width + 1]
        sums = sums[::2]

    before = jnp.zeros((1, 1), F32)
    for c in range(chunks):
        token = slice(c * CHUNK, (c + 1) * CHUNK)
        level_c = level[token, :]
        gates = gate[h : h + 1, token]
        gate_column = jnp.sum(jnp.where(rows == columns, gates, 0.0), axis=1, keepdims=True)
        column = jnp.sum(jnp.where(causal, gates, 0.0), axis=1, keepdims=True)
        row = jnp.sum(jnp.where(rows <= columns, gate_column, 0.0), axis=0, keepdims=True)
        query = query_rows[token, h * DH : (h + 1) * DH]
        query_f = query.astype(F32)
        scores = dot(query, kv[token, 2 * h * DH : (2 * h + 1) * DH], ((1,), (1,)))
        weights = jnp.take_along_axis(level_c, level_index, axis=1)
        decay = jnp.exp(jnp.where(causal, column - row, -1e30))
        lhs = [(weights * decay * scores).astype(BF16)]
        rhs = [kv[token, (2 * h + 1) * DH : (2 * h + 2) * DH]]
        chunk_level = level_c * jnp.exp(column)
        for bit in range(3):
            if (c, bit) in states:
                where = h * LEVELS + 8 + bit
                lhs.append((chunk_level[:, where : where + 1] * query_f).astype(BF16))
                rhs.append(states[c, bit])
        block_level = level_c * jnp.exp(column + before)
        for n in range(low_bits):
            where = h * LEVELS + 11 + n
            lhs.append((block_level[:, where : where + 1] * query_f).astype(BF16))
            rhs.append(low_states[n, h])
        inside[token, :] = dot(jnp.concatenate(lhs, axis=1), jnp.concatenate(rhs, axis=0))
        before = before + totals[c]


def scale_kernel(h, query_rows, level, gate, after, left):
    causal = iota(0) >= iota(1)
    before = jnp.zeros((1, 1), F32)
    for c in range(left.shape[0] // CHUNK):
        token = slice(c * CHUNK, (c + 1) * CHUNK)
        gates = gate[h : h + 1, token]
        column = jnp.sum(jnp.where(causal, gates, 0.0), axis=1, keepdims=True)
        block_level = level[token, :] * jnp.exp(column + before)
        query_f = query_rows[token, h * DH : (h + 1) * DH].astype(F32)
        for n in range(left.shape[1] // DH):
            where = h * LEVELS + 13 + n
            left[token, n * DH : (n + 1) * DH] = (
                block_level[:, where : where + 1] * query_f
            ).astype(BF16)
        before = before + jnp.sum(gates, axis=1, keepdims=True)


def within_kernel(place, own, two, one, three, after, states, onward, carry):
    pieces = (own, one, two, three)
    x = place[0]
    heads = states.shape[1]
    start = heads * DH + TAIL
    quarter = heads * DH // NX
    owner = [x ^ d for d in range(NX)]
    decays = [decays_of(piece, heads) for piece in pieces]
    group_decay = []
    carry[...] = jnp.zeros_like(carry)
    for h in range(heads):
        rows = slice(h * DH, (h + 1) * DH)
        bits = [jnp.zeros((DH, DH), F32) for _ in range(2)]
        before = jnp.zeros((1, DH), F32)
        whole = jnp.zeros((1, DH), F32)
        for d in range(NX):
            whole = whole + decays[d][h]
            before = before + jnp.where(owner[d] < x, decays[d][h], 0.0)
            if d == 0:
                continue
            piece = pieces[d][rows, :].astype(F32)
            to_here = jnp.zeros((1, DH), F32)
            for e in range(1, NX):
                after_it = (owner[e] > owner[d]) & (owner[e] < x)
                to_here = to_here + jnp.where(after_it, decays[e][h], 0.0)
            scale = jnp.where(owner[d] < x, jnp.exp(to_here), 0.0)
            for bit in range(2):
                used = (
                    (((x >> bit) & 1) == 1)
                    & (((owner[d] >> bit) & 1) == 0)
                    & ((x >> (bit + 1)) == (owner[d] >> (bit + 1)))
                )
                bits[bit] = bits[bit] + piece * jnp.where(used, scale, 0.0)
        for bit in range(2):
            states[bit, h] = bits[bit].astype(BF16)
        carry[h : h + 1, :] = before
        group_decay.append(whole)
    mine = pl.ds(pl.multiple_of(x * quarter, quarter), quarter)
    group = jnp.zeros((quarter, DH), F32)
    for d in range(NX):
        to_end = jnp.zeros((1, DH), F32)
        for e in range(NX):
            decay = jnp.where(x < NX // 2, decays[e][0], decays[e][1])
            to_end = to_end + jnp.where(owner[e] > owner[d], decay, 0.0)
        group = group + pieces[d][mine, :].astype(F32) * jnp.exp(to_end)
    onward[:quarter, :] = group.astype(BF16)
    onward[quarter : quarter + TAIL, :] = decay_rows(group_decay)
    prior = own[start:, :].astype(F32)
    for piece in pieces[1:]:
        prior = prior + piece[start:, :].astype(F32)
    onward[quarter + TAIL :, :] = prior.astype(BF16)


def halves_kernel(below, above, after, first, second, sems):
    size = first.shape[0]
    copies = [
        pltpu.make_async_copy(below.at[pl.ds(0, size), :], first, sems.at[0]),
        pltpu.make_async_copy(above.at[pl.ds(size, size), :], second, sems.at[1]),
    ]
    for copy in copies:
        copy.start()
    for copy in copies:
        copy.wait()


def pair_kernel(place, own, got, carry_in, after, state_out, onward, carry):
    x, z = place[0], place[1]
    heads = 2
    quarter = heads * DH // NX
    upper = (z & 1) == 1
    decay_own = tail_decays(own[quarter : quarter + TAIL, :], heads)
    decay_got = tail_decays(got[quarter : quarter + TAIL, :], heads)
    carry[...] = jnp.zeros_like(carry)
    for h in range(heads):
        before = carry_in[h : h + 1, :]
        carry[2 + h : 3 + h, :] = before
        carry[h : h + 1, :] = before + jnp.where(upper, decay_got[h], 0.0)
    state_out[...] = jnp.where(upper, got[:quarter, :].astype(F32), 0.0).astype(BF16)
    first = x < NX // 2
    mine = jnp.where(first, decay_own[0], decay_own[1])
    theirs = jnp.where(first, decay_got[0], decay_got[1])
    scale_own = jnp.where(upper, 1.0, jnp.exp(theirs))
    scale_got = jnp.where(upper, jnp.exp(mine), 1.0)
    total = own[:quarter, :].astype(F32) * scale_own + got[:quarter, :].astype(F32) * scale_got
    onward[:quarter, :] = total.astype(BF16)
    onward[quarter : quarter + TAIL, :] = decay_rows(
        [decay_own[h] + decay_got[h] for h in range(heads)]
    )
    prior = own[quarter + TAIL :, :].astype(F32) + got[quarter + TAIL :, :].astype(F32)
    onward[quarter + TAIL :, :] = prior.astype(BF16)


def pairs_kernel(place, own, far, skip, near, carry_in, low_state, after, payload, carry):
    x, z = place[0], place[1]
    heads = 2
    quarter = heads * DH // NX
    pair = z >> 1
    odd = (z & 1) == 1
    prior = slice(quarter + TAIL, own.shape[0])
    total = own[prior, :].astype(F32) + near[prior, :].astype(F32)
    total = total + skip[prior, :].astype(F32) + far[prior, :].astype(F32)

    def pick(flag, left, right):
        return jnp.where(flag, left, right)

    tail = slice(quarter, quarter + TAIL)
    tail_near, tail_skip = near[tail, :].astype(F32), skip[tail, :].astype(F32)
    decay_next = tail_decays(pick(odd, tail_near, tail_skip), heads)
    decay_prev = tail_decays(pick(odd, tail_skip, tail_near), heads)
    decay_far = tail_decays(far[tail, :], heads)
    carry[...] = carry_in[...]
    for h in range(heads):
        before = carry_in[h : h + 1, :]
        carry[4 + h : 5 + h, :] = before
        carry[6 + h : 7 + h, :] = before + pick(pair == 3, decay_prev[h], 0.0)
        offset = before + pick(pair >= 1, decay_prev[h], 0.0) + pick(pair >= 2, decay_far[h], 0.0)
        carry[h : h + 1, :] = offset + pick(pair == 3, decay_next[h], 0.0)
    state_near, state_skip = near[:quarter, :].astype(F32), skip[:quarter, :].astype(F32)
    state_next = pick(odd, state_near, state_skip)
    state_prev = pick(odd, state_skip, state_near)
    state_far = far[:quarter, :].astype(F32)
    first = x < NX // 2
    decay_one = pick(
        pair == 2,
        pick(first, decay_prev[0], decay_prev[1]),
        pick(first, decay_far[0], decay_far[1]),
    )
    zero_state = pick(pair == 2, state_far, state_next)
    one_state = pick(pair == 2, state_prev, state_far)
    high = pick(pair >= 2, zero_state * jnp.exp(decay_one) + one_state, 0.0)
    payload[:quarter, :] = low_state[...]
    payload[quarter : 2 * quarter, :] = pick((pair & 1) == 1, state_prev, 0.0).astype(BF16)
    payload[2 * quarter : 3 * quarter, :] = high.astype(BF16)
    payload[3 * quarter :, :] = total.astype(BF16)


def finish_kernel(place, carry, *refs):
    heads = 2
    insides, lefts, refs = refs[:heads], refs[heads : 2 * heads], refs[2 * heads :]
    own, two, one, three = refs[:NX]
    pieces, outs, states = (own, one, two, three), refs[NX:-1], refs[-1]
    z_bits = lefts[0].shape[1] // DH - PRIOR
    x = place[0]
    quarter = heads * DH // NX
    offsets = [jnp.exp(carry[h : h + 1, :]) for h in range(heads)]
    for d in range(NX):
        owner = x ^ d
        first = owner < NX // 2
        for bit in range(z_bits):
            before = jnp.where(first, carry[2 + 2 * bit : 3 + 2 * bit, :], carry[3 + 2 * bit : 4 + 2 * bit, :])
            piece = pieces[d][bit * quarter : (bit + 1) * quarter, :].astype(F32) * jnp.exp(before)
            where = bit * DH + lax.rem(owner, 2) * quarter
            states[owner // 2, pl.ds(pl.multiple_of(where, quarter), quarter), :] = piece.astype(BF16)
        for h in range(heads):
            rows = slice(z_bits * quarter + h * DH, z_bits * quarter + (h + 1) * DH)
            where = pl.multiple_of((z_bits + owner) * DH, DH)
            piece = pieces[d][rows, :].astype(F32) * offsets[h]
            states[h, pl.ds(where, DH), :] = piece.astype(BF16)
    rows_kernel((1, 3, 2), place, *insides, *lefts, states, *outs)


def rows_kernel(distances, place, *refs):
    heads = 2
    insides, lefts = refs[:heads], refs[heads : 2 * heads]
    states, outs = refs[2 * heads], refs[-len(distances) :]
    for d, out in zip(distances, outs):
        chip = place[2] ^ d
        token = pl.ds(pl.multiple_of(chip * TILE, TILE), TILE)
        for h in range(heads):
            u = insides[h][token, :] + dot(lefts[h][token, :], states[h])
            normed = u * lax.rsqrt(jnp.mean(u * u, axis=1, keepdims=True) + 1e-06)
            out[:, h * DH : (h + 1) * DH] = normed.astype(BF16)


def near_kernel(place, *refs):
    refs, (mine, theirs, rows) = refs[:-3], refs[-3:]
    pieces, weights = refs[: len(refs) // 2], refs[len(refs) // 2 :]

    @pl.when(pl.program_id(0) == 0)
    def _():
        for d, piece in enumerate(pieces):
            for side in range(2):
                where = pl.multiple_of((place[3] ^ side) * CHUNK, CHUNK)
                rows[d, side * CHUNK : (side + 1) * CHUNK, :] = piece[pl.ds(where, CHUNK), :]

    total = dot(rows[0], weights[0][...])
    for d in range(1, len(pieces)):
        total = total + dot(rows[d], weights[d][...])
    mine[...] = total[:CHUNK]
    theirs[...] = total[CHUNK:]


def far_kernel(side, place, piece, first, second, near, out):
    weight = jnp.concatenate([first[...], second[...]], axis=0)
    where = pl.multiple_of((place[3] ^ side) * CHUNK, CHUNK)
    total = near[...] + dot(piece[pl.ds(where, CHUNK), :], weight)
    out[...] = total.astype(out.dtype)


ANY = pl.BlockSpec(memory_space=pl.ANY)
HBM = pl.BlockSpec(memory_space=pltpu.HBM)


def small(kernel, shapes, *operands, specs=None, outs=None, scratch=(), flops=0, mib=24):
    return pl.pallas_call(
        kernel,
        out_shape=shapes,
        in_specs=specs or [SMEM if o.dtype == jnp.int32 else VMEM for o in operands],
        out_specs=outs or jax.tree.map(lambda _: VMEM, shapes),
        scratch_shapes=list(scratch),
        compiler_params=params(mib),
        cost_estimate=pl.CostEstimate(flops=flops, bytes_accessed=1 << 20, transcendentals=0),
    )(*operands)


def shards(activations, qkv_weight, level_proj, log_gate, prior_parts, out_weight):
    block, width = activations.shape
    heads = log_gate.shape[1]
    nz = lax.axis_size("ctx") // NX
    nh = lax.axis_size("head")
    ny = nh // 2
    z_bits = nz.bit_length() - 1
    chunks = block // CHUNK
    rows = heads * DH
    quarter = rows // NX
    shape = jax.ShapeDtypeStruct
    ctx = lax.axis_index("ctx").astype(jnp.int32)
    head = lax.axis_index("head").astype(jnp.int32)
    place = jnp.stack([ctx % NX, ctx // NX, head // 2, head % 2])

    def along_x(array, d):
        return lax.ppermute(
            array, "ctx", [(z * NX + x, z * NX + (x ^ d)) for z in range(nz) for x in range(NX)]
        )

    def across_z(array, target):
        return lax.ppermute(
            array, "ctx", [(z * NX + x, target(z) % nz * NX + x) for z in range(nz) for x in range(NX)]
        )

    def along_y(array, d):
        return lax.ppermute(
            array, "head", [(y * 2 + c, (y ^ d) * 2 + c) for y in range(ny) for c in range(2)]
        )

    below, above = along_y(out_weight, 1), along_y(out_weight, 3)
    gate = log_gate.T
    sent = shape((rows + TAIL + rows, DH), BF16)
    dma = pltpu.SemaphoreType.DMA
    kv, query_weight = small(
        keys_kernel,
        [shape((block, 2 * rows), BF16), shape((width, rows), BF16)],
        activations,
        qkv_weight,
        specs=[HBM] * 2,
        scratch=[
            pltpu.VMEM(activations.shape, BF16),
            pltpu.VMEM(qkv_weight.shape, BF16),
            dma((8,)),
            dma((8,)),
        ],
        flops=4 * block * width * rows,
        mib=50,
    )
    chunk_states, *payloads = small(
        states_kernel,
        [shape((chunks, heads, DH, DH), F32)] + [sent] * NX,
        place,
        kv,
        gate,
        prior_parts[0],
    )
    pieces = [payloads[0]] + [along_x(payloads[d], d) for d in range(1, NX)]

    query, level = small(
        level_kernel,
        [shape((block, rows), BF16), shape((block, DH), F32)],
        activations,
        query_weight,
        level_proj.T,
        payloads[0],
        specs=[VMEM] * 3 + [ANY],
        flops=4 * block * width * rows,
        mib=24,
    )

    def scaled(h, after):
        return small(
            functools.partial(scale_kernel, h),
            shape((block, (z_bits + PRIOR) * DH), BF16),
            query,
            level,
            gate,
            after,
            specs=[VMEM] * 3 + [ANY],
            flops=1 << 30,
        )

    lefts = [scaled(0, payloads[0])]
    low_states, onward, carry = small(
        within_kernel,
        [
            shape((2, heads, DH, DH), BF16),
            shape((quarter + TAIL + rows, DH), BF16),
            shape((8, DH), F32),
        ],
        place,
        pieces[0],
        pieces[2],
        pieces[1],
        pieces[3],
        lefts[0],
        specs=[SMEM] + [VMEM] * NX + [ANY],
    )

    def attend(h, after):
        return small(
            functools.partial(attend_kernel, h),
            shape((block, DH), F32),
            query,
            kv,
            level,
            gate,
            chunk_states,
            low_states,
            after,
            specs=[VMEM] * 6 + [ANY],
            flops=1 << 30,
        )

    got = across_z(onward, lambda z: z ^ 1)
    insides = [attend(0, onward)]
    state, onward, carry = small(
        pair_kernel,
        [shape((quarter, DH), BF16), shape(onward.shape, BF16), shape((8, DH), F32)],
        place,
        onward,
        got,
        carry,
        insides[0],
        specs=[SMEM] + [VMEM] * 3 + [ANY],
    )
    far = across_z(onward, lambda z: z + 3 if z % 2 else z - 3)
    skip = across_z(onward, lambda z: z + 2 if z % 2 else z - 2)
    near = across_z(onward, lambda z: z + 1 if z % 2 else z - 1)
    insides.append(attend(1, onward))
    halves = small(
        halves_kernel,
        [shape((rows // 2, width), BF16)] * 2,
        below,
        above,
        insides[1],
        specs=[ANY] * 3,
        outs=[VMEM] * 2,
        scratch=[dma((2,))],
        mib=4,
    )
    far_weight = along_y(halves[0], 3), along_y(halves[1], 1)
    payload, carry = small(
        pairs_kernel,
        [shape((z_bits * quarter + rows, DH), BF16), shape((8, DH), F32)],
        place,
        onward,
        far,
        skip,
        near,
        carry,
        state,
        halves[0],
        specs=[SMEM] + [VMEM] * 6 + [ANY],
    )
    lefts.append(scaled(1, payload))
    pieces = [payload] + [along_x(payload, d) for d in range(1, NX)]
    rows_out = shape((block // ny, rows), BF16)
    normed = [None] * ny
    normed[1], normed[3], normed[2], states = small(
        finish_kernel,
        [rows_out] * 3 + [shape((heads, (z_bits + PRIOR) * DH, DH), BF16)],
        place,
        carry,
        *insides,
        *lefts,
        pieces[0],
        pieces[2],
        pieces[1],
        pieces[3],
        flops=1 << 28,
    )
    normed[0] = small(
        functools.partial(rows_kernel, (0,)),
        rows_out,
        place,
        *insides,
        *lefts,
        states,
        normed[1],
        specs=[SMEM] + [VMEM] * 5 + [ANY],
        flops=1 << 28,
    )
    normed = [normed[0]] + [along_y(normed[d], d) for d in range(1, ny)]
    columns = 1024 if width % 1024 == 0 else width
    fixed = pl.BlockSpec((2 * CHUNK, rows), lambda i: (0, 0))
    weight_block = pl.BlockSpec((rows, columns), lambda i: (0, i))
    out_block = pl.BlockSpec((CHUNK, columns), lambda i: (0, i))
    half_block = pl.BlockSpec((rows // 2, columns), lambda i: (0, i))
    mine, theirs = pl.pallas_call(
        near_kernel,
        grid=(width // columns,),
        in_specs=[SMEM] + [fixed] * 3 + [weight_block] * 3,
        out_specs=[out_block] * 2,
        out_shape=[shape((CHUNK, width), F32)] * 2,
        scratch_shapes=[pltpu.VMEM((3, 2 * CHUNK, rows), BF16)],
        compiler_params=params(24),
        cost_estimate=pl.CostEstimate(flops=8 << 28, bytes_accessed=5 << 20, transcendentals=0),
    )(place, normed[0], normed[1], normed[3], out_weight, below, above)

    def add_far(side, near, dtype):
        return pl.pallas_call(
            functools.partial(far_kernel, side),
            grid=(width // columns,),
            in_specs=[SMEM, fixed, half_block, half_block, out_block],
            out_specs=out_block,
            out_shape=shape((CHUNK, width), dtype),
            compiler_params=params(24),
            cost_estimate=pl.CostEstimate(flops=1 << 28, bytes_accessed=3 << 20, transcendentals=0),
        )(place, normed[2], *far_weight, near)

    send = add_far(1, theirs, BF16)
    got = lax.ppermute(send, "head", [(i, i ^ 1) for i in range(nh)])
    keep = add_far(0, mine, F32)
    return (keep + got.astype(F32)).astype(BF16)


def solution(mesh):
    placed = (
        P("ctx", None),
        P(None, "head"),
        P(None, "head"),
        P("ctx", "head"),
        P("ctx", None, "head", None, None),
        P("head", None),
    )
    return jax.shard_map(
        shards, mesh=mesh, in_specs=placed, out_specs=P(("ctx", "head"), None), check_vma=False
    )
```

```python
import functools

import jax
import jax.numpy as jnp
from jax import lax
from jax.experimental import pallas as pl
from jax.experimental.pallas import tpu as pltpu
from jax.sharding import PartitionSpec as P

DH = 128
LEVELS = 21
PRIOR = 4
CHUNK = 128
TILE = 256
NX = 4
TAIL = 16
VMEM = pl.BlockSpec(memory_space=pltpu.VMEM)
SMEM = pl.BlockSpec(memory_space=pltpu.SMEM)
F32 = jnp.float32
BF16 = jnp.bfloat16


def params(mib=48):
    return pltpu.CompilerParams(vmem_limit_bytes=mib * 1024 * 1024)


def dot(left, right, contract=((1,), (0,))):
    return lax.dot_general(left, right, (contract, ((), ())), preferred_element_type=F32)


def iota(axis, shape=(CHUNK, CHUNK)):
    return lax.broadcasted_iota(jnp.int32, shape, axis)


def decay_rows(decays):
    rows = iota(0, (TAIL, DH))
    tail = jnp.zeros((TAIL, DH), F32)
    for index, decay in enumerate(decays):
        rest = jnp.broadcast_to(decay, (1, DH))
        for piece in range(3):
            part = rest.astype(BF16).astype(F32)
            tail = jnp.where(rows == index * 3 + piece, part, tail)
            rest = rest - part
    return tail.astype(BF16)


def tail_decays(tail, heads):
    tail = tail.astype(F32)
    return [
        (tail[3 * h : 3 * h + 1] + tail[3 * h + 1 : 3 * h + 2]) + tail[3 * h + 2 : 3 * h + 3]
        for h in range(heads)
    ]


def decays_of(payload, heads):
    return tail_decays(payload[heads * DH : heads * DH + TAIL, :], heads)


def copy_parts(source, target, sems):
    count = sems.shape[0]
    size = target.shape[0] // count
    copies = []
    for i in range(count):
        part = pl.ds(i * size, size)
        copies.append(pltpu.make_async_copy(source.at[part, :], target.at[part, :], sems.at[i]))
        copies[-1].start()
    return copies


def keys_kernel(acts_hbm, weight_hbm, kv, query_weight, acts, weight, weight_sem, acts_sem):
    block = acts.shape[0]
    heads = query_weight.shape[1] // DH
    weight_copies = copy_parts(weight_hbm, weight, weight_sem)
    acts_copies = copy_parts(acts_hbm, acts, acts_sem)
    for copy in weight_copies:
        copy.wait()
    per_tile = len(acts_copies) * TILE // block
    for i in range(block // TILE):
        for copy in acts_copies[i * per_tile : (i + 1) * per_tile]:
            copy.wait()
        token = slice(i * TILE, (i + 1) * TILE)
        for h in range(heads):
            both = dot(acts[token, :], weight[:, h * 3 * DH + DH : (h + 1) * 3 * DH])
            kv[token, h * 2 * DH : (h + 1) * 2 * DH] = both.astype(BF16)
    for h in range(heads):
        query_weight[:, h * DH : (h + 1) * DH] = weight[:, h * 3 * DH : h * 3 * DH + DH]


def states_kernel(place, kv, gate, prior, chunk_states, *payloads):
    x = place[0]
    heads, block = gate.shape
    later = iota(1) > iota(0)
    for h in range(heads):
        rows = slice(h * DH, (h + 1) * DH)
        total = None
        for c in range(block // CHUNK):
            token = slice(c * CHUNK, (c + 1) * CHUNK)
            gates = gate[h : h + 1, token]
            to_end = jnp.exp(jnp.sum(jnp.where(later, gates, 0.0), axis=1, keepdims=True))
            keys = kv[token, 2 * h * DH : (2 * h + 1) * DH].astype(F32)
            values = kv[token, (2 * h + 1) * DH : (2 * h + 2) * DH]
            state = dot((keys * to_end).astype(BF16), values, ((0,), (0,)))
            chunk_states[c, h] = state
            decay = jnp.exp(jnp.sum(gates, axis=1, keepdims=True))
            total = state if total is None else total * decay + state
        for payload in payloads:
            payload[rows, :] = total.astype(BF16)
    tail = decay_rows([jnp.sum(gate[h : h + 1, :], axis=1, keepdims=True) for h in range(heads)])
    start = heads * DH + TAIL
    for d, payload in enumerate(payloads):
        payload[heads * DH : start, :] = tail
        for h in range(heads):
            payload[start + h * DH : start + (h + 1) * DH, :] = prior[x ^ d, h].astype(BF16)


def level_kernel(acts, weight, proj, after, query, level):
    for i in range(acts.shape[0] // TILE):
        rows = slice(i * TILE, (i + 1) * TILE)
        query[rows, :] = dot(acts[rows, :], weight[...]).astype(BF16)
        raw = dot(acts[rows, :], proj[...], ((1,), (1,)))
        value = (jnp.maximum(raw, 0.0) + jnp.log1p(jnp.exp(-jnp.abs(raw)))) * DH ** (-0.5)
        pad = jnp.zeros((TILE, DH - value.shape[1]), F32)
        level[rows, :] = jnp.concatenate([value, pad], axis=1)


def attend_kernel(h, query_rows, kv, level, gate, chunk_states, low_states, after, inside):
    chunks = chunk_states.shape[0]
    low_bits = low_states.shape[0]
    rows, columns = iota(0), iota(1)
    causal = rows >= columns
    differing = jnp.bitwise_xor(rows, columns)
    level_index = jnp.full((CHUNK, CHUNK), h * LEVELS, jnp.int32)
    for bit in range(7):
        level_index = level_index + (differing >= (1 << bit)).astype(jnp.int32)

    totals = [
        jnp.sum(gate[h : h + 1, c * CHUNK : (c + 1) * CHUNK], axis=1, keepdims=True)
        for c in range(chunks)
    ]
    states = {}
    sums = [chunk_states[c, h] for c in range(chunks)]
    for bit in range(3):
        width = 1 << bit
        for low in range(0, chunks, 2 * width):
            state = sums[low // width]
            for c in range(low + width, low + 2 * width):
                states[c, bit] = state.astype(BF16)
                state = state * jnp.exp(totals[c])
            sums[low // width] = state + sums[low // width + 1]
        sums = sums[::2]

    before = jnp.zeros((1, 1), F32)
    for c in range(chunks):
        token = slice(c * CHUNK, (c + 1) * CHUNK)
        level_c = level[token, :]
        gates = gate[h : h + 1, token]
        gate_column = jnp.sum(jnp.where(rows == columns, gates, 0.0), axis=1, keepdims=True)
        column = jnp.sum(jnp.where(causal, gates, 0.0), axis=1, keepdims=True)
        row = jnp.sum(jnp.where(rows <= columns, gate_column, 0.0), axis=0, keepdims=True)
        query = query_rows[token, h * DH : (h + 1) * DH]
        query_f = query.astype(F32)
        scores = dot(query, kv[token, 2 * h * DH : (2 * h + 1) * DH], ((1,), (1,)))
        weights = jnp.take_along_axis(level_c, level_index, axis=1)
        decay = jnp.exp(jnp.where(causal, column - row, -1e30))
        lhs = [(weights * decay * scores).astype(BF16)]
        rhs = [kv[token, (2 * h + 1) * DH : (2 * h + 2) * DH]]
        chunk_level = level_c * jnp.exp(column)
        for bit in range(3):
            if (c, bit) in states:
                where = h * LEVELS + 8 + bit
                lhs.append((chunk_level[:, where : where + 1] * query_f).astype(BF16))
                rhs.append(states[c, bit])
        block_level = level_c * jnp.exp(column + before)
        for n in range(low_bits):
            where = h * LEVELS + 11 + n
            lhs.append((block_level[:, where : where + 1] * query_f).astype(BF16))
            rhs.append(low_states[n, h])
        inside[token, :] = dot(jnp.concatenate(lhs, axis=1), jnp.concatenate(rhs, axis=0))
        before = before + totals[c]


def scale_kernel(h, query_rows, level, gate, after, left):
    causal = iota(0) >= iota(1)
    before = jnp.zeros((1, 1), F32)
    for c in range(left.shape[0] // CHUNK):
        token = slice(c * CHUNK, (c + 1) * CHUNK)
        gates = gate[h : h + 1, token]
        column = jnp.sum(jnp.where(causal, gates, 0.0), axis=1, keepdims=True)
        block_level = level[token, :] * jnp.exp(column + before)
        query_f = query_rows[token, h * DH : (h + 1) * DH].astype(F32)
        for n in range(left.shape[1] // DH):
            where = h * LEVELS + 13 + n
            left[token, n * DH : (n + 1) * DH] = (
                block_level[:, where : where + 1] * query_f
            ).astype(BF16)
        before = before + jnp.sum(gates, axis=1, keepdims=True)


def within_kernel(place, own, two, one, three, after, states, onward, carry):
    pieces = (own, one, two, three)
    x = place[0]
    heads = states.shape[1]
    start = heads * DH + TAIL
    quarter = heads * DH // NX
    owner = [x ^ d for d in range(NX)]
    decays = [decays_of(piece, heads) for piece in pieces]
    group_decay = []
    carry[...] = jnp.zeros_like(carry)
    for h in range(heads):
        rows = slice(h * DH, (h + 1) * DH)
        bits = [jnp.zeros((DH, DH), F32) for _ in range(2)]
        before = jnp.zeros((1, DH), F32)
        whole = jnp.zeros((1, DH), F32)
        for d in range(NX):
            whole = whole + decays[d][h]
            before = before + jnp.where(owner[d] < x, decays[d][h], 0.0)
            if d == 0:
                continue
            piece = pieces[d][rows, :].astype(F32)
            to_here = jnp.zeros((1, DH), F32)
            for e in range(1, NX):
                after_it = (owner[e] > owner[d]) & (owner[e] < x)
                to_here = to_here + jnp.where(after_it, decays[e][h], 0.0)
            scale = jnp.where(owner[d] < x, jnp.exp(to_here), 0.0)
            for bit in range(2):
                used = (
                    (((x >> bit) & 1) == 1)
                    & (((owner[d] >> bit) & 1) == 0)
                    & ((x >> (bit + 1)) == (owner[d] >> (bit + 1)))
                )
                bits[bit] = bits[bit] + piece * jnp.where(used, scale, 0.0)
        for bit in range(2):
            states[bit, h] = bits[bit].astype(BF16)
        carry[h : h + 1, :] = before
        group_decay.append(whole)
    mine = pl.ds(pl.multiple_of(x * quarter, quarter), quarter)
    group = jnp.zeros((quarter, DH), F32)
    for d in range(NX):
        to_end = jnp.zeros((1, DH), F32)
        for e in range(NX):
            decay = jnp.where(x < NX // 2, decays[e][0], decays[e][1])
            to_end = to_end + jnp.where(owner[e] > owner[d], decay, 0.0)
        group = group + pieces[d][mine, :].astype(F32) * jnp.exp(to_end)
    onward[:quarter, :] = group.astype(BF16)
    onward[quarter : quarter + TAIL, :] = decay_rows(group_decay)
    prior = own[start:, :].astype(F32)
    for piece in pieces[1:]:
        prior = prior + piece[start:, :].astype(F32)
    onward[quarter + TAIL :, :] = prior.astype(BF16)


def halves_kernel(below, above, after, first, second, sems):
    size = first.shape[0]
    copies = [
        pltpu.make_async_copy(below.at[pl.ds(0, size), :], first, sems.at[0]),
        pltpu.make_async_copy(above.at[pl.ds(size, size), :], second, sems.at[1]),
    ]
    for copy in copies:
        copy.start()
    for copy in copies:
        copy.wait()


def pair_kernel(place, own, got, carry_in, after, state_out, onward, carry):
    x, z = place[0], place[1]
    heads = 2
    quarter = heads * DH // NX
    upper = (z & 1) == 1
    decay_own = tail_decays(own[quarter : quarter + TAIL, :], heads)
    decay_got = tail_decays(got[quarter : quarter + TAIL, :], heads)
    carry[...] = jnp.zeros_like(carry)
    for h in range(heads):
        before = carry_in[h : h + 1, :]
        carry[2 + h : 3 + h, :] = before
        carry[h : h + 1, :] = before + jnp.where(upper, decay_got[h], 0.0)
    state_out[...] = jnp.where(upper, got[:quarter, :].astype(F32), 0.0).astype(BF16)
    first = x < NX // 2
    mine = jnp.where(first, decay_own[0], decay_own[1])
    theirs = jnp.where(first, decay_got[0], decay_got[1])
    scale_own = jnp.where(upper, 1.0, jnp.exp(theirs))
    scale_got = jnp.where(upper, jnp.exp(mine), 1.0)
    total = own[:quarter, :].astype(F32) * scale_own + got[:quarter, :].astype(F32) * scale_got
    onward[:quarter, :] = total.astype(BF16)
    onward[quarter : quarter + TAIL, :] = decay_rows(
        [decay_own[h] + decay_got[h] for h in range(heads)]
    )
    prior = own[quarter + TAIL :, :].astype(F32) + got[quarter + TAIL :, :].astype(F32)
    onward[quarter + TAIL :, :] = prior.astype(BF16)


def pairs_kernel(place, own, far, skip, near, carry_in, low_state, after, payload, carry):
    x, z = place[0], place[1]
    heads = 2
    quarter = heads * DH // NX
    pair = z >> 1
    odd = (z & 1) == 1
    prior = slice(quarter + TAIL, own.shape[0])
    total = own[prior, :].astype(F32) + near[prior, :].astype(F32)
    total = total + skip[prior, :].astype(F32) + far[prior, :].astype(F32)

    def pick(flag, left, right):
        return jnp.where(flag, left, right)

    tail = slice(quarter, quarter + TAIL)
    tail_near, tail_skip = near[tail, :].astype(F32), skip[tail, :].astype(F32)
    decay_next = tail_decays(pick(odd, tail_near, tail_skip), heads)
    decay_prev = tail_decays(pick(odd, tail_skip, tail_near), heads)
    decay_far = tail_decays(far[tail, :], heads)
    carry[...] = carry_in[...]
    for h in range(heads):
        before = carry_in[h : h + 1, :]
        carry[4 + h : 5 + h, :] = before
        carry[6 + h : 7 + h, :] = before + pick(pair == 3, decay_prev[h], 0.0)
        offset = before + pick(pair >= 1, decay_prev[h], 0.0) + pick(pair >= 2, decay_far[h], 0.0)
        carry[h : h + 1, :] = offset + pick(pair == 3, decay_next[h], 0.0)
    state_near, state_skip = near[:quarter, :].astype(F32), skip[:quarter, :].astype(F32)
    state_next = pick(odd, state_near, state_skip)
    state_prev = pick(odd, state_skip, state_near)
    state_far = far[:quarter, :].astype(F32)
    first = x < NX // 2
    decay_one = pick(
        pair == 2,
        pick(first, decay_prev[0], decay_prev[1]),
        pick(first, decay_far[0], decay_far[1]),
    )
    zero_state = pick(pair == 2, state_far, state_next)
    one_state = pick(pair == 2, state_prev, state_far)
    high = pick(pair >= 2, zero_state * jnp.exp(decay_one) + one_state, 0.0)
    payload[:quarter, :] = low_state[...]
    payload[quarter : 2 * quarter, :] = pick((pair & 1) == 1, state_prev, 0.0).astype(BF16)
    payload[2 * quarter : 3 * quarter, :] = high.astype(BF16)
    payload[3 * quarter :, :] = total.astype(BF16)


def finish_kernel(place, carry, *refs):
    heads = 2
    insides, lefts, refs = refs[:heads], refs[heads : 2 * heads], refs[2 * heads :]
    own, one, two, three = refs[:NX]
    pieces, outs, states = (own, one, two, three), refs[NX:-1], refs[-1]
    z_bits = lefts[0].shape[1] // DH - PRIOR
    x = place[0]
    quarter = heads * DH // NX
    offsets = [jnp.exp(carry[h : h + 1, :]) for h in range(heads)]
    for d in range(NX):
        owner = x ^ d
        first = owner < NX // 2
        for bit in range(z_bits):
            before = jnp.where(first, carry[2 + 2 * bit : 3 + 2 * bit, :], carry[3 + 2 * bit : 4 + 2 * bit, :])
            piece = pieces[d][bit * quarter : (bit + 1) * quarter, :].astype(F32) * jnp.exp(before)
            where = bit * DH + lax.rem(owner, 2) * quarter
            states[owner // 2, pl.ds(pl.multiple_of(where, quarter), quarter), :] = piece.astype(BF16)
        for h in range(heads):
            rows = slice(z_bits * quarter + h * DH, z_bits * quarter + (h + 1) * DH)
            where = pl.multiple_of((z_bits + owner) * DH, DH)
            piece = pieces[d][rows, :].astype(F32) * offsets[h]
            states[h, pl.ds(where, DH), :] = piece.astype(BF16)
    rows_kernel((1, 3, 2), place, *insides, *lefts, states, *outs)


def rows_kernel(distances, place, *refs):
    heads = 2
    insides, lefts = refs[:heads], refs[heads : 2 * heads]
    states, outs = refs[2 * heads], refs[-len(distances) :]
    for d, out in zip(distances, outs):
        chip = place[2] ^ d
        token = pl.ds(pl.multiple_of(chip * TILE, TILE), TILE)
        for h in range(heads):
            u = insides[h][token, :] + dot(lefts[h][token, :], states[h])
            normed = u * lax.rsqrt(jnp.mean(u * u, axis=1, keepdims=True) + 1e-06)
            out[:, h * DH : (h + 1) * DH] = normed.astype(BF16)


def near_kernel(place, *refs):
    refs, (mine, theirs, rows) = refs[:-3], refs[-3:]
    pieces, weights = refs[: len(refs) // 2], refs[len(refs) // 2 :]

    @pl.when(pl.program_id(0) == 0)
    def _():
        for d, piece in enumerate(pieces):
            for side in range(2):
                where = pl.multiple_of((place[3] ^ side) * CHUNK, CHUNK)
                rows[d, side * CHUNK : (side + 1) * CHUNK, :] = piece[pl.ds(where, CHUNK), :]

    total = dot(rows[0], weights[0][...])
    for d in range(1, len(pieces)):
        total = total + dot(rows[d], weights[d][...])
    mine[...] = total[:CHUNK]
    theirs[...] = total[CHUNK:]


def far_kernel(side, place, piece, first, second, near, out):
    weight = jnp.concatenate([first[...], second[...]], axis=0)
    where = pl.multiple_of((place[3] ^ side) * CHUNK, CHUNK)
    total = near[...] + dot(piece[pl.ds(where, CHUNK), :], weight)
    out[...] = total.astype(out.dtype)


ANY = pl.BlockSpec(memory_space=pl.ANY)
HBM = pl.BlockSpec(memory_space=pltpu.HBM)


def small(kernel, shapes, *operands, specs=None, outs=None, scratch=(), flops=0, mib=24):
    return pl.pallas_call(
        kernel,
        out_shape=shapes,
        in_specs=specs or [SMEM if o.dtype == jnp.int32 else VMEM for o in operands],
        out_specs=outs or jax.tree.map(lambda _: VMEM, shapes),
        scratch_shapes=list(scratch),
        compiler_params=params(mib),
        cost_estimate=pl.CostEstimate(flops=flops, bytes_accessed=1 << 20, transcendentals=0),
    )(*operands)


def shards(activations, qkv_weight, level_proj, log_gate, prior_parts, out_weight):
    block, width = activations.shape
    heads = log_gate.shape[1]
    nz = lax.axis_size("ctx") // NX
    nh = lax.axis_size("head")
    ny = nh // 2
    z_bits = nz.bit_length() - 1
    chunks = block // CHUNK
    rows = heads * DH
    quarter = rows // NX
    shape = jax.ShapeDtypeStruct
    ctx = lax.axis_index("ctx").astype(jnp.int32)
    head = lax.axis_index("head").astype(jnp.int32)
    place = jnp.stack([ctx % NX, ctx // NX, head // 2, head % 2])

    def along_x(array, d):
        return lax.ppermute(
            array, "ctx", [(z * NX + x, z * NX + (x ^ d)) for z in range(nz) for x in range(NX)]
        )

    def across_z(array, target):
        return lax.ppermute(
            array, "ctx", [(z * NX + x, target(z) % nz * NX + x) for z in range(nz) for x in range(NX)]
        )

    def along_y(array, d):
        return lax.ppermute(
            array, "head", [(y * 2 + c, (y ^ d) * 2 + c) for y in range(ny) for c in range(2)]
        )

    below, above = along_y(out_weight, 1), along_y(out_weight, 3)
    gate = log_gate.T
    sent = shape((rows + TAIL + rows, DH), BF16)
    dma = pltpu.SemaphoreType.DMA
    kv, query_weight = small(
        keys_kernel,
        [shape((block, 2 * rows), BF16), shape((width, rows), BF16)],
        activations,
        qkv_weight,
        specs=[HBM] * 2,
        scratch=[
            pltpu.VMEM(activations.shape, BF16),
            pltpu.VMEM(qkv_weight.shape, BF16),
            dma((8,)),
            dma((8,)),
        ],
        flops=4 * block * width * rows,
        mib=50,
    )
    chunk_states, *payloads = small(
        states_kernel,
        [shape((chunks, heads, DH, DH), F32)] + [sent] * NX,
        place,
        kv,
        gate,
        prior_parts[0],
    )
    pieces = [payloads[0]] + [along_x(payloads[d], d) for d in range(1, NX)]

    query, level = small(
        level_kernel,
        [shape((block, rows), BF16), shape((block, DH), F32)],
        activations,
        query_weight,
        level_proj.T,
        payloads[0],
        specs=[VMEM] * 3 + [ANY],
        flops=4 * block * width * rows,
        mib=24,
    )

    def scaled(h, after):
        return small(
            functools.partial(scale_kernel, h),
            shape((block, (z_bits + PRIOR) * DH), BF16),
            query,
            level,
            gate,
            after,
            specs=[VMEM] * 3 + [ANY],
            flops=1 << 30,
        )

    lefts = [scaled(0, payloads[0])]
    low_states, onward, carry = small(
        within_kernel,
        [
            shape((2, heads, DH, DH), BF16),
            shape((quarter + TAIL + rows, DH), BF16),
            shape((8, DH), F32),
        ],
        place,
        pieces[0],
        pieces[2],
        pieces[1],
        pieces[3],
        lefts[0],
        specs=[SMEM] + [VMEM] * NX + [ANY],
    )

    def attend(h, after):
        return small(
            functools.partial(attend_kernel, h),
            shape((block, DH), F32),
            query,
            kv,
            level,
            gate,
            chunk_states,
            low_states,
            after,
            specs=[VMEM] * 6 + [ANY],
            flops=1 << 30,
        )

    got = across_z(onward, lambda z: z ^ 1)
    insides = [attend(0, onward)]
    state, onward, carry = small(
        pair_kernel,
        [shape((quarter, DH), BF16), shape(onward.shape, BF16), shape((8, DH), F32)],
        place,
        onward,
        got,
        carry,
        insides[0],
        specs=[SMEM] + [VMEM] * 3 + [ANY],
    )
    far = across_z(onward, lambda z: z + 3 if z % 2 else z - 3)
    skip = across_z(onward, lambda z: z + 2 if z % 2 else z - 2)
    near = across_z(onward, lambda z: z + 1 if z % 2 else z - 1)
    insides.append(attend(1, onward))
    halves = small(
        halves_kernel,
        [shape((rows // 2, width), BF16)] * 2,
        below,
        above,
        insides[1],
        specs=[ANY] * 3,
        outs=[VMEM] * 2,
        scratch=[dma((2,))],
        mib=4,
    )
    far_weight = along_y(halves[0], 3), along_y(halves[1], 1)
    payload, carry = small(
        pairs_kernel,
        [shape((z_bits * quarter + rows, DH), BF16), shape((8, DH), F32)],
        place,
        onward,
        far,
        skip,
        near,
        carry,
        state,
        halves[0],
        specs=[SMEM] + [VMEM] * 6 + [ANY],
    )
    lefts.append(scaled(1, payload))
    pieces = [payload] + [along_x(payload, d) for d in range(1, NX)]
    rows_out = shape((block // ny, rows), BF16)
    normed = [None] * ny
    normed[1], normed[3], normed[2], states = small(
        finish_kernel,
        [rows_out] * 3 + [shape((heads, (z_bits + PRIOR) * DH, DH), BF16)],
        place,
        carry,
        *insides,
        *lefts,
        pieces[0],
        pieces[1],
        pieces[2],
        pieces[3],
        flops=1 << 28,
    )
    normed[0] = small(
        functools.partial(rows_kernel, (0,)),
        rows_out,
        place,
        *insides,
        *lefts,
        states,
        normed[1],
        specs=[SMEM] + [VMEM] * 5 + [ANY],
        flops=1 << 28,
    )
    normed = [normed[0]] + [along_y(normed[d], d) for d in range(1, ny)]
    columns = 1024 if width % 1024 == 0 else width
    fixed = pl.BlockSpec((2 * CHUNK, rows), lambda i: (0, 0))
    weight_block = pl.BlockSpec((rows, columns), lambda i: (0, i))
    out_block = pl.BlockSpec((CHUNK, columns), lambda i: (0, i))
    half_block = pl.BlockSpec((rows // 2, columns), lambda i: (0, i))
    mine, theirs = pl.pallas_call(
        near_kernel,
        grid=(width // columns,),
        in_specs=[SMEM] + [fixed] * 3 + [weight_block] * 3,
        out_specs=[out_block] * 2,
        out_shape=[shape((CHUNK, width), F32)] * 2,
        scratch_shapes=[pltpu.VMEM((3, 2 * CHUNK, rows), BF16)],
        compiler_params=params(24),
        cost_estimate=pl.CostEstimate(flops=8 << 28, bytes_accessed=5 << 20, transcendentals=0),
    )(place, normed[0], normed[3], normed[1], out_weight, above, below)

    def add_far(side, near, dtype):
        return pl.pallas_call(
            functools.partial(far_kernel, side),
            grid=(width // columns,),
            in_specs=[SMEM, fixed, half_block, half_block, out_block],
            out_specs=out_block,
            out_shape=shape((CHUNK, width), dtype),
            compiler_params=params(24),
            cost_estimate=pl.CostEstimate(flops=1 << 28, bytes_accessed=3 << 20, transcendentals=0),
        )(place, normed[2], *far_weight, near)

    send = add_far(1, theirs, BF16)
    got = lax.ppermute(send, "head", [(i, i ^ 1) for i in range(nh)])
    keep = add_far(0, mine, F32)
    return (keep + got.astype(F32)).astype(BF16)


def solution(mesh):
    placed = (
        P("ctx", None),
        P(None, "head"),
        P(None, "head"),
        P("ctx", "head"),
        P("ctx", None, "head", None, None),
        P("head", None),
    )
    return jax.shard_map(
        shards, mesh=mesh, in_specs=placed, out_specs=P(("ctx", "head"), None), check_vma=False
    )
```

```python
import functools

import jax
import jax.numpy as jnp
from jax import lax
from jax.experimental import pallas as pl
from jax.experimental.pallas import tpu as pltpu
from jax.sharding import PartitionSpec as P

DH = 128
LEVELS = 21
PRIOR = 4
CHUNK = 128
TILE = 256
NX = 4
TAIL = 16
VMEM = pl.BlockSpec(memory_space=pltpu.VMEM)
SMEM = pl.BlockSpec(memory_space=pltpu.SMEM)
F32 = jnp.float32
BF16 = jnp.bfloat16


def params(mib=48):
    return pltpu.CompilerParams(vmem_limit_bytes=mib * 1024 * 1024)


def dot(left, right, contract=((1,), (0,))):
    return lax.dot_general(left, right, (contract, ((), ())), preferred_element_type=F32)


def iota(axis, shape=(CHUNK, CHUNK)):
    return lax.broadcasted_iota(jnp.int32, shape, axis)


def decay_rows(decays):
    rows = iota(0, (TAIL, DH))
    tail = jnp.zeros((TAIL, DH), F32)
    for index, decay in enumerate(decays):
        rest = jnp.broadcast_to(decay, (1, DH))
        for piece in range(3):
            part = rest.astype(BF16).astype(F32)
            tail = jnp.where(rows == index * 3 + piece, part, tail)
            rest = rest - part
    return tail.astype(BF16)


def tail_decays(tail, heads):
    tail = tail.astype(F32)
    return [
        (tail[3 * h : 3 * h + 1] + tail[3 * h + 1 : 3 * h + 2]) + tail[3 * h + 2 : 3 * h + 3]
        for h in range(heads)
    ]


def decays_of(payload, heads):
    return tail_decays(payload[heads * DH : heads * DH + TAIL, :], heads)


def copy_parts(source, target, sems):
    count = sems.shape[0]
    size = target.shape[0] // count
    copies = []
    for i in range(count):
        part = pl.ds(i * size, size)
        copies.append(pltpu.make_async_copy(source.at[part, :], target.at[part, :], sems.at[i]))
        copies[-1].start(priority=1)
    return copies


def keys_kernel(acts_hbm, weight_hbm, kv, query_weight, acts, weight, weight_sem, acts_sem):
    block = acts.shape[0]
    heads = query_weight.shape[1] // DH
    weight_copies = copy_parts(weight_hbm, weight, weight_sem)
    acts_copies = copy_parts(acts_hbm, acts, acts_sem)
    for copy in weight_copies:
        copy.wait()
    per_tile = len(acts_copies) * TILE // block
    for i in range(block // TILE):
        for copy in acts_copies[i * per_tile : (i + 1) * per_tile]:
            copy.wait()
        token = slice(i * TILE, (i + 1) * TILE)
        for h in range(heads):
            both = dot(acts[token, :], weight[:, h * 3 * DH + DH : (h + 1) * 3 * DH])
            kv[token, h * 2 * DH : (h + 1) * 2 * DH] = both.astype(BF16)
    for h in range(heads):
        query_weight[:, h * DH : (h + 1) * DH] = weight[:, h * 3 * DH : h * 3 * DH + DH]


def states_kernel(place, kv, gate, prior, chunk_states, *payloads):
    x = place[0]
    heads, block = gate.shape
    later = iota(1) > iota(0)
    for h in range(heads):
        rows = slice(h * DH, (h + 1) * DH)
        total = None
        for c in range(block // CHUNK):
            token = slice(c * CHUNK, (c + 1) * CHUNK)
            gates = gate[h : h + 1, token]
            to_end = jnp.exp(jnp.sum(jnp.where(later, gates, 0.0), axis=1, keepdims=True))
            keys = kv[token, 2 * h * DH : (2 * h + 1) * DH].astype(F32)
            values = kv[token, (2 * h + 1) * DH : (2 * h + 2) * DH]
            state = dot((keys * to_end).astype(BF16), values, ((0,), (0,)))
            chunk_states[c, h] = state
            decay = jnp.exp(jnp.sum(gates, axis=1, keepdims=True))
            total = state if total is None else total * decay + state
        for payload in payloads:
            payload[rows, :] = total.astype(BF16)
    tail = decay_rows([jnp.sum(gate[h : h + 1, :], axis=1, keepdims=True) for h in range(heads)])
    start = heads * DH + TAIL
    for d, payload in enumerate(payloads):
        payload[heads * DH : start, :] = tail
        for h in range(heads):
            payload[start + h * DH : start + (h + 1) * DH, :] = prior[x ^ d, h].astype(BF16)


def level_kernel(acts, weight, proj, after, query, level):
    for i in range(acts.shape[0] // TILE):
        rows = slice(i * TILE, (i + 1) * TILE)
        query[rows, :] = dot(acts[rows, :], weight[...]).astype(BF16)
        raw = dot(acts[rows, :], proj[...], ((1,), (1,)))
        value = (jnp.maximum(raw, 0.0) + jnp.log1p(jnp.exp(-jnp.abs(raw)))) * DH ** (-0.5)
        pad = jnp.zeros((TILE, DH - value.shape[1]), F32)
        level[rows, :] = jnp.concatenate([value, pad], axis=1)


def attend_kernel(h, query_rows, kv, level, gate, chunk_states, low_states, after, inside):
    chunks = chunk_states.shape[0]
    low_bits = low_states.shape[0]
    rows, columns = iota(0), iota(1)
    causal = rows >= columns
    differing = jnp.bitwise_xor(rows, columns)
    level_index = jnp.full((CHUNK, CHUNK), h * LEVELS, jnp.int32)
    for bit in range(7):
        level_index = level_index + (differing >= (1 << bit)).astype(jnp.int32)

    totals = [
        jnp.sum(gate[h : h + 1, c * CHUNK : (c + 1) * CHUNK], axis=1, keepdims=True)
        for c in range(chunks)
    ]
    states = {}
    sums = [chunk_states[c, h] for c in range(chunks)]
    for bit in range(3):
        width = 1 << bit
        for low in range(0, chunks, 2 * width):
            state = sums[low // width]
            for c in range(low + width, low + 2 * width):
                states[c, bit] = state.astype(BF16)
                state = state * jnp.exp(totals[c])
            sums[low // width] = state + sums[low // width + 1]
        sums = sums[::2]

    before = jnp.zeros((1, 1), F32)
    for c in range(chunks):
        token = slice(c * CHUNK, (c + 1) * CHUNK)
        level_c = level[token, :]
        gates = gate[h : h + 1, token]
        gate_column = jnp.sum(jnp.where(rows == columns, gates, 0.0), axis=1, keepdims=True)
        column = jnp.sum(jnp.where(causal, gates, 0.0), axis=1, keepdims=True)
        row = jnp.sum(jnp.where(rows <= columns, gate_column, 0.0), axis=0, keepdims=True)
        query = query_rows[token, h * DH : (h + 1) * DH]
        query_f = query.astype(F32)
        scores = dot(query, kv[token, 2 * h * DH : (2 * h + 1) * DH], ((1,), (1,)))
        weights = jnp.take_along_axis(level_c, level_index, axis=1)
        decay = jnp.exp(jnp.where(causal, column - row, -1e30))
        lhs = [(weights * decay * scores).astype(BF16)]
        rhs = [kv[token, (2 * h + 1) * DH : (2 * h + 2) * DH]]
        chunk_level = level_c * jnp.exp(column)
        for bit in range(3):
            if (c, bit) in states:
                where = h * LEVELS + 8 + bit
                lhs.append((chunk_level[:, where : where + 1] * query_f).astype(BF16))
                rhs.append(states[c, bit])
        block_level = level_c * jnp.exp(column + before)
        for n in range(low_bits):
            where = h * LEVELS + 11 + n
            lhs.append((block_level[:, where : where + 1] * query_f).astype(BF16))
            rhs.append(low_states[n, h])
        inside[token, :] = dot(jnp.concatenate(lhs, axis=1), jnp.concatenate(rhs, axis=0))
        before = before + totals[c]


def scale_kernel(h, query_rows, level, gate, after, left):
    causal = iota(0) >= iota(1)
    before = jnp.zeros((1, 1), F32)
    for c in range(left.shape[0] // CHUNK):
        token = slice(c * CHUNK, (c + 1) * CHUNK)
        gates = gate[h : h + 1, token]
        column = jnp.sum(jnp.where(causal, gates, 0.0), axis=1, keepdims=True)
        block_level = level[token, :] * jnp.exp(column + before)
        query_f = query_rows[token, h * DH : (h + 1) * DH].astype(F32)
        for n in range(left.shape[1] // DH):
            where = h * LEVELS + 13 + n
            left[token, n * DH : (n + 1) * DH] = (
                block_level[:, where : where + 1] * query_f
            ).astype(BF16)
        before = before + jnp.sum(gates, axis=1, keepdims=True)


def within_kernel(place, own, two, one, three, after, states, onward, carry):
    pieces = (own, one, two, three)
    x = place[0]
    heads = states.shape[1]
    start = heads * DH + TAIL
    quarter = heads * DH // NX
    owner = [x ^ d for d in range(NX)]
    decays = [decays_of(piece, heads) for piece in pieces]
    group_decay = []
    carry[...] = jnp.zeros_like(carry)
    for h in range(heads):
        rows = slice(h * DH, (h + 1) * DH)
        bits = [jnp.zeros((DH, DH), F32) for _ in range(2)]
        before = jnp.zeros((1, DH), F32)
        whole = jnp.zeros((1, DH), F32)
        for d in range(NX):
            whole = whole + decays[d][h]
            before = before + jnp.where(owner[d] < x, decays[d][h], 0.0)
            if d == 0:
                continue
            piece = pieces[d][rows, :].astype(F32)
            to_here = jnp.zeros((1, DH), F32)
            for e in range(1, NX):
                after_it = (owner[e] > owner[d]) & (owner[e] < x)
                to_here = to_here + jnp.where(after_it, decays[e][h], 0.0)
            scale = jnp.where(owner[d] < x, jnp.exp(to_here), 0.0)
            for bit in range(2):
                used = (
                    (((x >> bit) & 1) == 1)
                    & (((owner[d] >> bit) & 1) == 0)
                    & ((x >> (bit + 1)) == (owner[d] >> (bit + 1)))
                )
                bits[bit] = bits[bit] + piece * jnp.where(used, scale, 0.0)
        for bit in range(2):
            states[bit, h] = bits[bit].astype(BF16)
        carry[h : h + 1, :] = before
        group_decay.append(whole)
    mine = pl.ds(pl.multiple_of(x * quarter, quarter), quarter)
    group = jnp.zeros((quarter, DH), F32)
    for d in range(NX):
        to_end = jnp.zeros((1, DH), F32)
        for e in range(NX):
            decay = jnp.where(x < NX // 2, decays[e][0], decays[e][1])
            to_end = to_end + jnp.where(owner[e] > owner[d], decay, 0.0)
        group = group + pieces[d][mine, :].astype(F32) * jnp.exp(to_end)
    onward[:quarter, :] = group.astype(BF16)
    onward[quarter : quarter + TAIL, :] = decay_rows(group_decay)
    prior = own[start:, :].astype(F32)
    for piece in pieces[1:]:
        prior = prior + piece[start:, :].astype(F32)
    onward[quarter + TAIL :, :] = prior.astype(BF16)


def halves_kernel(below, above, after, first, second, sems):
    size = first.shape[0]
    copies = [
        pltpu.make_async_copy(below.at[pl.ds(0, size), :], first, sems.at[0]),
        pltpu.make_async_copy(above.at[pl.ds(size, size), :], second, sems.at[1]),
    ]
    for copy in copies:
        copy.start()
    for copy in copies:
        copy.wait()


def pair_kernel(place, own, got, carry_in, after, state_out, onward, carry):
    x, z = place[0], place[1]
    heads = 2
    quarter = heads * DH // NX
    upper = (z & 1) == 1
    decay_own = tail_decays(own[quarter : quarter + TAIL, :], heads)
    decay_got = tail_decays(got[quarter : quarter + TAIL, :], heads)
    carry[...] = jnp.zeros_like(carry)
    for h in range(heads):
        before = carry_in[h : h + 1, :]
        carry[2 + h : 3 + h, :] = before
        carry[h : h + 1, :] = before + jnp.where(upper, decay_got[h], 0.0)
    state_out[...] = jnp.where(upper, got[:quarter, :].astype(F32), 0.0).astype(BF16)
    first = x < NX // 2
    mine = jnp.where(first, decay_own[0], decay_own[1])
    theirs = jnp.where(first, decay_got[0], decay_got[1])
    scale_own = jnp.where(upper, 1.0, jnp.exp(theirs))
    scale_got = jnp.where(upper, jnp.exp(mine), 1.0)
    total = own[:quarter, :].astype(F32) * scale_own + got[:quarter, :].astype(F32) * scale_got
    onward[:quarter, :] = total.astype(BF16)
    onward[quarter : quarter + TAIL, :] = decay_rows(
        [decay_own[h] + decay_got[h] for h in range(heads)]
    )
    prior = own[quarter + TAIL :, :].astype(F32) + got[quarter + TAIL :, :].astype(F32)
    onward[quarter + TAIL :, :] = prior.astype(BF16)


def pairs_kernel(place, own, far, skip, near, carry_in, low_state, after, payload, carry):
    x, z = place[0], place[1]
    heads = 2
    quarter = heads * DH // NX
    pair = z >> 1
    odd = (z & 1) == 1
    prior = slice(quarter + TAIL, own.shape[0])
    total = own[prior, :].astype(F32) + near[prior, :].astype(F32)
    total = total + skip[prior, :].astype(F32) + far[prior, :].astype(F32)

    def pick(flag, left, right):
        return jnp.where(flag, left, right)

    tail = slice(quarter, quarter + TAIL)
    tail_near, tail_skip = near[tail, :].astype(F32), skip[tail, :].astype(F32)
    decay_next = tail_decays(pick(odd, tail_near, tail_skip), heads)
    decay_prev = tail_decays(pick(odd, tail_skip, tail_near), heads)
    decay_far = tail_decays(far[tail, :], heads)
    carry[...] = carry_in[...]
    for h in range(heads):
        before = carry_in[h : h + 1, :]
        carry[4 + h : 5 + h, :] = before
        carry[6 + h : 7 + h, :] = before + pick(pair == 3, decay_prev[h], 0.0)
        offset = before + pick(pair >= 1, decay_prev[h], 0.0) + pick(pair >= 2, decay_far[h], 0.0)
        carry[h : h + 1, :] = offset + pick(pair == 3, decay_next[h], 0.0)
    state_near, state_skip = near[:quarter, :].astype(F32), skip[:quarter, :].astype(F32)
    state_next = pick(odd, state_near, state_skip)
    state_prev = pick(odd, state_skip, state_near)
    state_far = far[:quarter, :].astype(F32)
    first = x < NX // 2
    decay_one = pick(
        pair == 2,
        pick(first, decay_prev[0], decay_prev[1]),
        pick(first, decay_far[0], decay_far[1]),
    )
    zero_state = pick(pair == 2, state_far, state_next)
    one_state = pick(pair == 2, state_prev, state_far)
    high = pick(pair >= 2, zero_state * jnp.exp(decay_one) + one_state, 0.0)
    payload[:quarter, :] = low_state[...]
    payload[quarter : 2 * quarter, :] = pick((pair & 1) == 1, state_prev, 0.0).astype(BF16)
    payload[2 * quarter : 3 * quarter, :] = high.astype(BF16)
    payload[3 * quarter :, :] = total.astype(BF16)


def finish_kernel(place, carry, *refs):
    heads = 2
    insides, lefts, refs = refs[:heads], refs[heads : 2 * heads], refs[2 * heads :]
    own, one, two, three = refs[:NX]
    pieces, outs, states = (own, one, two, three), refs[NX:-1], refs[-1]
    z_bits = lefts[0].shape[1] // DH - PRIOR
    x = place[0]
    quarter = heads * DH // NX
    offsets = [jnp.exp(carry[h : h + 1, :]) for h in range(heads)]
    for d in range(NX):
        owner = x ^ d
        first = owner < NX // 2
        for bit in range(z_bits):
            before = jnp.where(first, carry[2 + 2 * bit : 3 + 2 * bit, :], carry[3 + 2 * bit : 4 + 2 * bit, :])
            piece = pieces[d][bit * quarter : (bit + 1) * quarter, :].astype(F32) * jnp.exp(before)
            where = bit * DH + lax.rem(owner, 2) * quarter
            states[owner // 2, pl.ds(pl.multiple_of(where, quarter), quarter), :] = piece.astype(BF16)
        for h in range(heads):
            rows = slice(z_bits * quarter + h * DH, z_bits * quarter + (h + 1) * DH)
            where = pl.multiple_of((z_bits + owner) * DH, DH)
            piece = pieces[d][rows, :].astype(F32) * offsets[h]
            states[h, pl.ds(where, DH), :] = piece.astype(BF16)
    rows_kernel((1, 3, 2), place, *insides, *lefts, states, *outs)


def rows_kernel(distances, place, *refs):
    heads = 2
    insides, lefts = refs[:heads], refs[heads : 2 * heads]
    states, outs = refs[2 * heads], refs[-len(distances) :]
    for d, out in zip(distances, outs):
        chip = place[2] ^ d
        token = pl.ds(pl.multiple_of(chip * TILE, TILE), TILE)
        for h in range(heads):
            u = insides[h][token, :] + dot(lefts[h][token, :], states[h])
            normed = u * lax.rsqrt(jnp.mean(u * u, axis=1, keepdims=True) + 1e-06)
            out[:, h * DH : (h + 1) * DH] = normed.astype(BF16)


def near_kernel(place, *refs):
    refs, (mine, theirs, rows) = refs[:-3], refs[-3:]
    pieces, weights = refs[: len(refs) // 2], refs[len(refs) // 2 :]

    @pl.when(pl.program_id(0) == 0)
    def _():
        for d, piece in enumerate(pieces):
            for side in range(2):
                where = pl.multiple_of((place[3] ^ side) * CHUNK, CHUNK)
                rows[d, side * CHUNK : (side + 1) * CHUNK, :] = piece[pl.ds(where, CHUNK), :]

    total = dot(rows[0], weights[0][...])
    for d in range(1, len(pieces)):
        total = total + dot(rows[d], weights[d][...])
    mine[...] = total[:CHUNK]
    theirs[...] = total[CHUNK:]


def far_kernel(side, place, piece, first, second, near, out):
    weight = jnp.concatenate([first[...], second[...]], axis=0)
    where = pl.multiple_of((place[3] ^ side) * CHUNK, CHUNK)
    total = near[...] + dot(piece[pl.ds(where, CHUNK), :], weight)
    out[...] = total.astype(out.dtype)


ANY = pl.BlockSpec(memory_space=pl.ANY)
HBM = pl.BlockSpec(memory_space=pltpu.HBM)


def small(kernel, shapes, *operands, specs=None, outs=None, scratch=(), flops=0, mib=24):
    return pl.pallas_call(
        kernel,
        out_shape=shapes,
        in_specs=specs or [SMEM if o.dtype == jnp.int32 else VMEM for o in operands],
        out_specs=outs or jax.tree.map(lambda _: VMEM, shapes),
        scratch_shapes=list(scratch),
        compiler_params=params(mib),
        cost_estimate=pl.CostEstimate(flops=flops, bytes_accessed=1 << 20, transcendentals=0),
    )(*operands)


def shards(activations, qkv_weight, level_proj, log_gate, prior_parts, out_weight):
    block, width = activations.shape
    heads = log_gate.shape[1]
    nz = lax.axis_size("ctx") // NX
    nh = lax.axis_size("head")
    ny = nh // 2
    z_bits = nz.bit_length() - 1
    chunks = block // CHUNK
    rows = heads * DH
    quarter = rows // NX
    shape = jax.ShapeDtypeStruct
    ctx = lax.axis_index("ctx").astype(jnp.int32)
    head = lax.axis_index("head").astype(jnp.int32)
    place = jnp.stack([ctx % NX, ctx // NX, head // 2, head % 2])

    def along_x(array, d):
        return lax.ppermute(
            array, "ctx", [(z * NX + x, z * NX + (x ^ d)) for z in range(nz) for x in range(NX)]
        )

    def across_z(array, target):
        return lax.ppermute(
            array, "ctx", [(z * NX + x, target(z) % nz * NX + x) for z in range(nz) for x in range(NX)]
        )

    def along_y(array, d):
        return lax.ppermute(
            array, "head", [(y * 2 + c, (y ^ d) * 2 + c) for y in range(ny) for c in range(2)]
        )

    below, above = along_y(out_weight, 1), along_y(out_weight, 3)
    gate = log_gate.T
    sent = shape((rows + TAIL + rows, DH), BF16)
    dma = pltpu.SemaphoreType.DMA
    kv, query_weight = small(
        keys_kernel,
        [shape((block, 2 * rows), BF16), shape((width, rows), BF16)],
        activations,
        qkv_weight,
        specs=[HBM] * 2,
        scratch=[
            pltpu.VMEM(activations.shape, BF16),
            pltpu.VMEM(qkv_weight.shape, BF16),
            dma((8,)),
            dma((8,)),
        ],
        flops=4 * block * width * rows,
        mib=50,
    )
    chunk_states, *payloads = small(
        states_kernel,
        [shape((chunks, heads, DH, DH), F32)] + [sent] * NX,
        place,
        kv,
        gate,
        prior_parts[0],
    )
    pieces = [payloads[0]] + [along_x(payloads[d], d) for d in range(1, NX)]

    query, level = small(
        level_kernel,
        [shape((block, rows), BF16), shape((block, DH), F32)],
        activations,
        query_weight,
        level_proj.T,
        payloads[0],
        specs=[VMEM] * 3 + [ANY],
        flops=4 * block * width * rows,
        mib=24,
    )

    def scaled(h, after):
        return small(
            functools.partial(scale_kernel, h),
            shape((block, (z_bits + PRIOR) * DH), BF16),
            query,
            level,
            gate,
            after,
            specs=[VMEM] * 3 + [ANY],
            flops=1 << 30,
        )

    lefts = [scaled(0, payloads[0])]
    low_states, onward, carry = small(
        within_kernel,
        [
            shape((2, heads, DH, DH), BF16),
            shape((quarter + TAIL + rows, DH), BF16),
            shape((8, DH), F32),
        ],
        place,
        pieces[0],
        pieces[2],
        pieces[1],
        pieces[3],
        lefts[0],
        specs=[SMEM] + [VMEM] * NX + [ANY],
    )

    def attend(h, after):
        return small(
            functools.partial(attend_kernel, h),
            shape((block, DH), F32),
            query,
            kv,
            level,
            gate,
            chunk_states,
            low_states,
            after,
            specs=[VMEM] * 6 + [ANY],
            flops=1 << 30,
        )

    got = across_z(onward, lambda z: z ^ 1)
    insides = [attend(0, onward)]
    state, onward, carry = small(
        pair_kernel,
        [shape((quarter, DH), BF16), shape(onward.shape, BF16), shape((8, DH), F32)],
        place,
        onward,
        got,
        carry,
        insides[0],
        specs=[SMEM] + [VMEM] * 3 + [ANY],
    )
    far = across_z(onward, lambda z: z + 3 if z % 2 else z - 3)
    skip = across_z(onward, lambda z: z + 2 if z % 2 else z - 2)
    near = across_z(onward, lambda z: z + 1 if z % 2 else z - 1)
    insides.append(attend(1, onward))
    halves = small(
        halves_kernel,
        [shape((rows // 2, width), BF16)] * 2,
        below,
        above,
        insides[1],
        specs=[ANY] * 3,
        outs=[VMEM] * 2,
        scratch=[dma((2,))],
        mib=4,
    )
    far_weight = along_y(halves[0], 3), along_y(halves[1], 1)
    payload, carry = small(
        pairs_kernel,
        [shape((z_bits * quarter + rows, DH), BF16), shape((8, DH), F32)],
        place,
        onward,
        far,
        skip,
        near,
        carry,
        state,
        halves[0],
        specs=[SMEM] + [VMEM] * 6 + [ANY],
    )
    lefts.append(scaled(1, payload))
    pieces = [payload] + [along_x(payload, d) for d in range(1, NX)]
    rows_out = shape((block // ny, rows), BF16)
    normed = [None] * ny
    normed[1], normed[3], normed[2], states = small(
        finish_kernel,
        [rows_out] * 3 + [shape((heads, (z_bits + PRIOR) * DH, DH), BF16)],
        place,
        carry,
        *insides,
        *lefts,
        pieces[0],
        pieces[1],
        pieces[2],
        pieces[3],
        flops=1 << 28,
    )
    normed[0] = small(
        functools.partial(rows_kernel, (0,)),
        rows_out,
        place,
        *insides,
        *lefts,
        states,
        normed[1],
        specs=[SMEM] + [VMEM] * 5 + [ANY],
        flops=1 << 28,
    )
    normed = [normed[0]] + [along_y(normed[d], d) for d in range(1, ny)]
    columns = 1024 if width % 1024 == 0 else width
    fixed = pl.BlockSpec((2 * CHUNK, rows), lambda i: (0, 0))
    weight_block = pl.BlockSpec((rows, columns), lambda i: (0, i))
    out_block = pl.BlockSpec((CHUNK, columns), lambda i: (0, i))
    half_block = pl.BlockSpec((rows // 2, columns), lambda i: (0, i))
    mine, theirs = pl.pallas_call(
        near_kernel,
        grid=(width // columns,),
        in_specs=[SMEM] + [fixed] * 3 + [weight_block] * 3,
        out_specs=[out_block] * 2,
        out_shape=[shape((CHUNK, width), F32)] * 2,
        scratch_shapes=[pltpu.VMEM((3, 2 * CHUNK, rows), BF16)],
        compiler_params=params(24),
        cost_estimate=pl.CostEstimate(flops=8 << 28, bytes_accessed=5 << 20, transcendentals=0),
    )(place, normed[0], normed[3], normed[1], out_weight, above, below)

    def add_far(side, near, dtype):
        return pl.pallas_call(
            functools.partial(far_kernel, side),
            grid=(width // columns,),
            in_specs=[SMEM, fixed, half_block, half_block, out_block],
            out_specs=out_block,
            out_shape=shape((CHUNK, width), dtype),
            compiler_params=params(24),
            cost_estimate=pl.CostEstimate(flops=1 << 28, bytes_accessed=3 << 20, transcendentals=0),
        )(place, normed[2], *far_weight, near)

    send = add_far(1, theirs, BF16)
    got = lax.ppermute(send, "head", [(i, i ^ 1) for i in range(nh)])
    keep = add_far(0, mine, F32)
    return (keep + got.astype(F32)).astype(BF16)


def solution(mesh):
    placed = (
        P("ctx", None),
        P(None, "head"),
        P(None, "head"),
        P("ctx", "head"),
        P("ctx", None, "head", None, None),
        P("head", None),
    )
    return jax.shard_map(
        shards, mesh=mesh, in_specs=placed, out_specs=P(("ctx", "head"), None), check_vma=False
    )
```

```python
import functools

import jax
import jax.numpy as jnp
from jax import lax
from jax.experimental import pallas as pl
from jax.experimental.pallas import tpu as pltpu
from jax.sharding import PartitionSpec as P

DH = 128
LEVELS = 21
PRIOR = 4
CHUNK = 128
TILE = 256
NX = 4
TAIL = 16
VMEM = pl.BlockSpec(memory_space=pltpu.VMEM)
SMEM = pl.BlockSpec(memory_space=pltpu.SMEM)
F32 = jnp.float32
BF16 = jnp.bfloat16


def params(mib=48):
    return pltpu.CompilerParams(vmem_limit_bytes=mib * 1024 * 1024)


def dot(left, right, contract=((1,), (0,))):
    return lax.dot_general(left, right, (contract, ((), ())), preferred_element_type=F32)


def iota(axis, shape=(CHUNK, CHUNK)):
    return lax.broadcasted_iota(jnp.int32, shape, axis)


def decay_rows(decays):
    rows = iota(0, (TAIL, DH))
    tail = jnp.zeros((TAIL, DH), F32)
    for index, decay in enumerate(decays):
        rest = jnp.broadcast_to(decay, (1, DH))
        for piece in range(3):
            part = rest.astype(BF16).astype(F32)
            tail = jnp.where(rows == index * 3 + piece, part, tail)
            rest = rest - part
    return tail.astype(BF16)


def tail_decays(tail, heads):
    tail = tail.astype(F32)
    return [
        (tail[3 * h : 3 * h + 1] + tail[3 * h + 1 : 3 * h + 2]) + tail[3 * h + 2 : 3 * h + 3]
        for h in range(heads)
    ]


def decays_of(payload, heads):
    return tail_decays(payload[heads * DH : heads * DH + TAIL, :], heads)


def copy_parts(source, target, sems):
    count = sems.shape[0]
    size = target.shape[0] // count
    copies = []
    for i in range(count):
        part = pl.ds(i * size, size)
        copies.append(pltpu.make_async_copy(source.at[part, :], target.at[part, :], sems.at[i]))
        copies[-1].start()
    return copies


def keys_kernel(acts_hbm, weight_hbm, kv, query_weight, acts, weight, weight_sem, acts_sem):
    block = acts.shape[0]
    heads = query_weight.shape[1] // DH
    weight_copies = copy_parts(weight_hbm, weight, weight_sem)
    acts_copies = copy_parts(acts_hbm, acts, acts_sem)
    for copy in weight_copies:
        copy.wait()
    per_tile = len(acts_copies) * TILE // block
    for i in range(block // TILE):
        for copy in acts_copies[i * per_tile : (i + 1) * per_tile]:
            copy.wait()
        token = slice(i * TILE, (i + 1) * TILE)
        for h in range(heads):
            both = dot(acts[token, :], weight[:, h * 3 * DH + DH : (h + 1) * 3 * DH])
            kv[token, h * 2 * DH : (h + 1) * 2 * DH] = both.astype(BF16)
    for h in range(heads):
        query_weight[:, h * DH : (h + 1) * DH] = weight[:, h * 3 * DH : h * 3 * DH + DH]


def states_kernel(place, kv, gate, prior, chunk_states, *payloads):
    x = place[0]
    heads, block = gate.shape
    later = iota(1) > iota(0)
    for h in range(heads):
        rows = slice(h * DH, (h + 1) * DH)
        total = None
        for c in range(block // CHUNK):
            token = slice(c * CHUNK, (c + 1) * CHUNK)
            gates = gate[h : h + 1, token]
            to_end = jnp.exp(jnp.sum(jnp.where(later, gates, 0.0), axis=1, keepdims=True))
            keys = kv[token, 2 * h * DH : (2 * h + 1) * DH].astype(F32)
            values = kv[token, (2 * h + 1) * DH : (2 * h + 2) * DH]
            state = dot((keys * to_end).astype(BF16), values, ((0,), (0,)))
            chunk_states[c, h] = state
            decay = jnp.exp(jnp.sum(gates, axis=1, keepdims=True))
            total = state if total is None else total * decay + state
        for payload in payloads:
            payload[rows, :] = total.astype(BF16)
    tail = decay_rows([jnp.sum(gate[h : h + 1, :], axis=1, keepdims=True) for h in range(heads)])
    start = heads * DH + TAIL
    for d, payload in enumerate(payloads):
        payload[heads * DH : start, :] = tail
        for h in range(heads):
            payload[start + h * DH : start + (h + 1) * DH, :] = prior[x ^ d, h].astype(BF16)


def level_kernel(acts, weight, proj, after, query, level):
    for i in range(acts.shape[0] // TILE):
        rows = slice(i * TILE, (i + 1) * TILE)
        query[rows, :] = dot(acts[rows, :], weight[...]).astype(BF16)
        raw = dot(acts[rows, :], proj[...], ((1,), (1,)))
        value = (jnp.maximum(raw, 0.0) + jnp.log1p(jnp.exp(-jnp.abs(raw)))) * DH ** (-0.5)
        pad = jnp.zeros((TILE, DH - value.shape[1]), F32)
        level[rows, :] = jnp.concatenate([value, pad], axis=1)


def attend_kernel(h, query_rows, kv, level, gate, chunk_states, low_states, after, inside):
    chunks = chunk_states.shape[0]
    low_bits = low_states.shape[0]
    rows, columns = iota(0), iota(1)
    causal = rows >= columns
    differing = jnp.bitwise_xor(rows, columns)
    level_index = jnp.full((CHUNK, CHUNK), h * LEVELS, jnp.int32)
    for bit in range(7):
        level_index = level_index + (differing >= (1 << bit)).astype(jnp.int32)

    totals = [
        jnp.sum(gate[h : h + 1, c * CHUNK : (c + 1) * CHUNK], axis=1, keepdims=True)
        for c in range(chunks)
    ]
    states = {}
    sums = [chunk_states[c, h] for c in range(chunks)]
    for bit in range(3):
        width = 1 << bit
        for low in range(0, chunks, 2 * width):
            state = sums[low // width]
            for c in range(low + width, low + 2 * width):
                states[c, bit] = state.astype(BF16)
                state = state * jnp.exp(totals[c])
            sums[low // width] = state + sums[low // width + 1]
        sums = sums[::2]

    before = jnp.zeros((1, 1), F32)
    for c in range(chunks):
        token = slice(c * CHUNK, (c + 1) * CHUNK)
        level_c = level[token, :]
        gates = gate[h : h + 1, token]
        gate_column = jnp.sum(jnp.where(rows == columns, gates, 0.0), axis=1, keepdims=True)
        column = jnp.sum(jnp.where(causal, gates, 0.0), axis=1, keepdims=True)
        row = jnp.sum(jnp.where(rows <= columns, gate_column, 0.0), axis=0, keepdims=True)
        query = query_rows[token, h * DH : (h + 1) * DH]
        query_f = query.astype(F32)
        scores = dot(query, kv[token, 2 * h * DH : (2 * h + 1) * DH], ((1,), (1,)))
        weights = jnp.take_along_axis(level_c, level_index, axis=1)
        decay = jnp.exp(jnp.where(causal, column - row, -1e30))
        lhs = [(weights * decay * scores).astype(BF16)]
        rhs = [kv[token, (2 * h + 1) * DH : (2 * h + 2) * DH]]
        chunk_level = level_c * jnp.exp(column)
        for bit in range(3):
            if (c, bit) in states:
                where = h * LEVELS + 8 + bit
                lhs.append((chunk_level[:, where : where + 1] * query_f).astype(BF16))
                rhs.append(states[c, bit])
        block_level = level_c * jnp.exp(column + before)
        for n in range(low_bits):
            where = h * LEVELS + 11 + n
            lhs.append((block_level[:, where : where + 1] * query_f).astype(BF16))
            rhs.append(low_states[n, h])
        inside[token, :] = dot(jnp.concatenate(lhs, axis=1), jnp.concatenate(rhs, axis=0))
        before = before + totals[c]


def scale_kernel(h, query_rows, level, gate, after, left):
    causal = iota(0) >= iota(1)
    before = jnp.zeros((1, 1), F32)
    for c in range(left.shape[0] // CHUNK):
        token = slice(c * CHUNK, (c + 1) * CHUNK)
        gates = gate[h : h + 1, token]
        column = jnp.sum(jnp.where(causal, gates, 0.0), axis=1, keepdims=True)
        block_level = level[token, :] * jnp.exp(column + before)
        query_f = query_rows[token, h * DH : (h + 1) * DH].astype(F32)
        for n in range(left.shape[1] // DH):
            where = h * LEVELS + 13 + n
            left[token, n * DH : (n + 1) * DH] = (
                block_level[:, where : where + 1] * query_f
            ).astype(BF16)
        before = before + jnp.sum(gates, axis=1, keepdims=True)


def within_kernel(place, own, two, one, three, after, states, onward, carry):
    pieces = (own, one, two, three)
    x = place[0]
    heads = states.shape[1]
    start = heads * DH + TAIL
    quarter = heads * DH // NX
    owner = [x ^ d for d in range(NX)]
    decays = [decays_of(piece, heads) for piece in pieces]
    group_decay = []
    carry[...] = jnp.zeros_like(carry)
    for h in range(heads):
        rows = slice(h * DH, (h + 1) * DH)
        bits = [jnp.zeros((DH, DH), F32) for _ in range(2)]
        before = jnp.zeros((1, DH), F32)
        whole = jnp.zeros((1, DH), F32)
        for d in range(NX):
            whole = whole + decays[d][h]
            before = before + jnp.where(owner[d] < x, decays[d][h], 0.0)
            if d == 0:
                continue
            piece = pieces[d][rows, :].astype(F32)
            to_here = jnp.zeros((1, DH), F32)
            for e in range(1, NX):
                after_it = (owner[e] > owner[d]) & (owner[e] < x)
                to_here = to_here + jnp.where(after_it, decays[e][h], 0.0)
            scale = jnp.where(owner[d] < x, jnp.exp(to_here), 0.0)
            for bit in range(2):
                used = (
                    (((x >> bit) & 1) == 1)
                    & (((owner[d] >> bit) & 1) == 0)
                    & ((x >> (bit + 1)) == (owner[d] >> (bit + 1)))
                )
                bits[bit] = bits[bit] + piece * jnp.where(used, scale, 0.0)
        for bit in range(2):
            states[bit, h] = bits[bit].astype(BF16)
        carry[h : h + 1, :] = before
        group_decay.append(whole)
    mine = pl.ds(pl.multiple_of(x * quarter, quarter), quarter)
    group = jnp.zeros((quarter, DH), F32)
    for d in range(NX):
        to_end = jnp.zeros((1, DH), F32)
        for e in range(NX):
            decay = jnp.where(x < NX // 2, decays[e][0], decays[e][1])
            to_end = to_end + jnp.where(owner[e] > owner[d], decay, 0.0)
        group = group + pieces[d][mine, :].astype(F32) * jnp.exp(to_end)
    onward[:quarter, :] = group.astype(BF16)
    onward[quarter : quarter + TAIL, :] = decay_rows(group_decay)
    prior = own[start:, :].astype(F32)
    for piece in pieces[1:]:
        prior = prior + piece[start:, :].astype(F32)
    onward[quarter + TAIL :, :] = prior.astype(BF16)


def halves_kernel(below, above, after, first, second, sems):
    size = first.shape[0]
    copies = [
        pltpu.make_async_copy(below.at[pl.ds(0, size), :], first, sems.at[0]),
        pltpu.make_async_copy(above.at[pl.ds(size, size), :], second, sems.at[1]),
    ]
    for copy in copies:
        copy.start()
    for copy in copies:
        copy.wait()


def pair_kernel(place, own, got, carry_in, after, state_out, onward, carry):
    x, z = place[0], place[1]
    heads = 2
    quarter = heads * DH // NX
    upper = (z & 1) == 1
    decay_own = tail_decays(own[quarter : quarter + TAIL, :], heads)
    decay_got = tail_decays(got[quarter : quarter + TAIL, :], heads)
    carry[...] = jnp.zeros_like(carry)
    for h in range(heads):
        before = carry_in[h : h + 1, :]
        carry[2 + h : 3 + h, :] = before
        carry[h : h + 1, :] = before + jnp.where(upper, decay_got[h], 0.0)
    state_out[...] = jnp.where(upper, got[:quarter, :].astype(F32), 0.0).astype(BF16)
    first = x < NX // 2
    mine = jnp.where(first, decay_own[0], decay_own[1])
    theirs = jnp.where(first, decay_got[0], decay_got[1])
    scale_own = jnp.where(upper, 1.0, jnp.exp(theirs))
    scale_got = jnp.where(upper, jnp.exp(mine), 1.0)
    total = own[:quarter, :].astype(F32) * scale_own + got[:quarter, :].astype(F32) * scale_got
    onward[:quarter, :] = total.astype(BF16)
    onward[quarter : quarter + TAIL, :] = decay_rows(
        [decay_own[h] + decay_got[h] for h in range(heads)]
    )
    prior = own[quarter + TAIL :, :].astype(F32) + got[quarter + TAIL :, :].astype(F32)
    onward[quarter + TAIL :, :] = prior.astype(BF16)


def pairs_kernel(place, own, far, skip, near, carry_in, low_state, after, payload, carry):
    x, z = place[0], place[1]
    heads = 2
    quarter = heads * DH // NX
    pair = z >> 1
    odd = (z & 1) == 1
    prior = slice(quarter + TAIL, own.shape[0])
    total = own[prior, :].astype(F32) + near[prior, :].astype(F32)
    total = total + skip[prior, :].astype(F32) + far[prior, :].astype(F32)

    def pick(flag, left, right):
        return jnp.where(flag, left, right)

    tail = slice(quarter, quarter + TAIL)
    tail_near, tail_skip = near[tail, :].astype(F32), skip[tail, :].astype(F32)
    decay_next = tail_decays(pick(odd, tail_near, tail_skip), heads)
    decay_prev = tail_decays(pick(odd, tail_skip, tail_near), heads)
    decay_far = tail_decays(far[tail, :], heads)
    carry[...] = carry_in[...]
    for h in range(heads):
        before = carry_in[h : h + 1, :]
        carry[4 + h : 5 + h, :] = before
        carry[6 + h : 7 + h, :] = before + pick(pair == 3, decay_prev[h], 0.0)
        offset = before + pick(pair >= 1, decay_prev[h], 0.0) + pick(pair >= 2, decay_far[h], 0.0)
        carry[h : h + 1, :] = offset + pick(pair == 3, decay_next[h], 0.0)
    state_near, state_skip = near[:quarter, :].astype(F32), skip[:quarter, :].astype(F32)
    state_next = pick(odd, state_near, state_skip)
    state_prev = pick(odd, state_skip, state_near)
    state_far = far[:quarter, :].astype(F32)
    first = x < NX // 2
    decay_one = pick(
        pair == 2,
        pick(first, decay_prev[0], decay_prev[1]),
        pick(first, decay_far[0], decay_far[1]),
    )
    zero_state = pick(pair == 2, state_far, state_next)
    one_state = pick(pair == 2, state_prev, state_far)
    high = pick(pair >= 2, zero_state * jnp.exp(decay_one) + one_state, 0.0)
    payload[:quarter, :] = low_state[...]
    payload[quarter : 2 * quarter, :] = pick((pair & 1) == 1, state_prev, 0.0).astype(BF16)
    payload[2 * quarter : 3 * quarter, :] = high.astype(BF16)
    payload[3 * quarter :, :] = total.astype(BF16)


def finish_kernel(place, carry, *refs):
    heads = 2
    insides, lefts, refs = refs[:heads], refs[heads : 2 * heads], refs[2 * heads :]
    own, one, two, three = refs[:NX]
    pieces, outs, states = (own, one, two, three), refs[NX:-1], refs[-1]
    z_bits = lefts[0].shape[1] // DH - PRIOR
    x = place[0]
    quarter = heads * DH // NX
    offsets = [jnp.exp(carry[h : h + 1, :]) for h in range(heads)]
    for d in range(NX):
        owner = x ^ d
        first = owner < NX // 2
        for bit in range(z_bits):
            before = jnp.where(first, carry[2 + 2 * bit : 3 + 2 * bit, :], carry[3 + 2 * bit : 4 + 2 * bit, :])
            piece = pieces[d][bit * quarter : (bit + 1) * quarter, :].astype(F32) * jnp.exp(before)
            where = bit * DH + lax.rem(owner, 2) * quarter
            states[owner // 2, pl.ds(pl.multiple_of(where, quarter), quarter), :] = piece.astype(BF16)
        for h in range(heads):
            rows = slice(z_bits * quarter + h * DH, z_bits * quarter + (h + 1) * DH)
            where = pl.multiple_of((z_bits + owner) * DH, DH)
            piece = pieces[d][rows, :].astype(F32) * offsets[h]
            states[h, pl.ds(where, DH), :] = piece.astype(BF16)
    rows_kernel((1, 3, 2), place, *insides, *lefts, states, *outs)


def rows_kernel(distances, place, *refs):
    heads = 2
    insides, lefts = refs[:heads], refs[heads : 2 * heads]
    states, outs = refs[2 * heads], refs[-len(distances) :]
    for d, out in zip(distances, outs):
        chip = place[2] ^ d
        token = pl.ds(pl.multiple_of(chip * TILE, TILE), TILE)
        for h in range(heads):
            u = insides[h][token, :] + dot(lefts[h][token, :], states[h])
            normed = u * lax.rsqrt(jnp.mean(u * u, axis=1, keepdims=True) + 1e-06)
            out[:, h * DH : (h + 1) * DH] = normed.astype(BF16)


def near_kernel(place, *refs):
    refs, (mine, theirs, rows) = refs[:-3], refs[-3:]
    pieces, weights = refs[: len(refs) // 2], refs[len(refs) // 2 :]

    @pl.when(pl.program_id(0) == 0)
    def _():
        for d, piece in enumerate(pieces):
            for side in range(2):
                where = pl.multiple_of((place[3] ^ side) * CHUNK, CHUNK)
                rows[d, side * CHUNK : (side + 1) * CHUNK, :] = piece[pl.ds(where, CHUNK), :]

    total = dot(rows[0], weights[0][...])
    for d in range(1, len(pieces)):
        total = total + dot(rows[d], weights[d][...])
    mine[...] = total[:CHUNK]
    theirs[...] = total[CHUNK:]


def far_kernel(side, place, piece, first, second, near, out):
    weight = jnp.concatenate([first[...], second[...]], axis=0)
    where = pl.multiple_of((place[3] ^ side) * CHUNK, CHUNK)
    total = near[...] + dot(piece[pl.ds(where, CHUNK), :], weight)
    out[...] = total.astype(out.dtype)


ANY = pl.BlockSpec(memory_space=pl.ANY)
HBM = pl.BlockSpec(memory_space=pltpu.HBM)


def small(kernel, shapes, *operands, specs=None, outs=None, scratch=(), flops=0, mib=24):
    return pl.pallas_call(
        kernel,
        out_shape=shapes,
        in_specs=specs or [SMEM if o.dtype == jnp.int32 else VMEM for o in operands],
        out_specs=outs or jax.tree.map(lambda _: VMEM, shapes),
        scratch_shapes=list(scratch),
        compiler_params=params(mib),
        cost_estimate=pl.CostEstimate(flops=flops, bytes_accessed=1 << 20, transcendentals=0),
    )(*operands)


def shards(activations, qkv_weight, level_proj, log_gate, prior_parts, out_weight):
    block, width = activations.shape
    heads = log_gate.shape[1]
    nz = lax.axis_size("ctx") // NX
    nh = lax.axis_size("head")
    ny = nh // 2
    z_bits = nz.bit_length() - 1
    chunks = block // CHUNK
    rows = heads * DH
    quarter = rows // NX
    shape = jax.ShapeDtypeStruct
    ctx = lax.axis_index("ctx").astype(jnp.int32)
    head = lax.axis_index("head").astype(jnp.int32)
    place = jnp.stack([ctx % NX, ctx // NX, head // 2, head % 2])

    def along_x(array, d):
        return lax.ppermute(
            array, "ctx", [(z * NX + x, z * NX + (x ^ d)) for z in range(nz) for x in range(NX)]
        )

    def across_z(array, target):
        return lax.ppermute(
            array, "ctx", [(z * NX + x, target(z) % nz * NX + x) for z in range(nz) for x in range(NX)]
        )

    def along_y(array, d):
        return lax.ppermute(
            array, "head", [(y * 2 + c, (y ^ d) * 2 + c) for y in range(ny) for c in range(2)]
        )

    below, above = along_y(out_weight, 1), along_y(out_weight, 3)
    gate = log_gate.T
    sent = shape((rows + TAIL + rows, DH), BF16)
    dma = pltpu.SemaphoreType.DMA
    kv, query_weight = small(
        keys_kernel,
        [shape((block, 2 * rows), BF16), shape((width, rows), BF16)],
        activations,
        qkv_weight,
        specs=[HBM] * 2,
        scratch=[
            pltpu.VMEM(activations.shape, BF16),
            pltpu.VMEM(qkv_weight.shape, BF16),
            dma((8,)),
            dma((8,)),
        ],
        flops=4 * block * width * rows,
        mib=50,
    )
    chunk_states, *payloads = small(
        states_kernel,
        [shape((chunks, heads, DH, DH), F32)] + [sent] * NX,
        place,
        kv,
        gate,
        prior_parts[0],
        flops=1 << 32,
    )
    pieces = [payloads[0]] + [along_x(payloads[d], d) for d in range(1, NX)]

    query, level = small(
        level_kernel,
        [shape((block, rows), BF16), shape((block, DH), F32)],
        activations,
        query_weight,
        level_proj.T,
        payloads[0],
        specs=[VMEM] * 3 + [ANY],
        flops=4 * block * width * rows,
        mib=24,
    )

    def scaled(h, after):
        return small(
            functools.partial(scale_kernel, h),
            shape((block, (z_bits + PRIOR) * DH), BF16),
            query,
            level,
            gate,
            after,
            specs=[VMEM] * 3 + [ANY],
            flops=1 << 30,
        )

    lefts = [scaled(0, payloads[0])]
    low_states, onward, carry = small(
        within_kernel,
        [
            shape((2, heads, DH, DH), BF16),
            shape((quarter + TAIL + rows, DH), BF16),
            shape((8, DH), F32),
        ],
        place,
        pieces[0],
        pieces[2],
        pieces[1],
        pieces[3],
        lefts[0],
        specs=[SMEM] + [VMEM] * NX + [ANY],
    )

    def attend(h, after):
        return small(
            functools.partial(attend_kernel, h),
            shape((block, DH), F32),
            query,
            kv,
            level,
            gate,
            chunk_states,
            low_states,
            after,
            specs=[VMEM] * 6 + [ANY],
            flops=1 << 30,
        )

    got = across_z(onward, lambda z: z ^ 1)
    insides = [attend(0, onward)]
    state, onward, carry = small(
        pair_kernel,
        [shape((quarter, DH), BF16), shape(onward.shape, BF16), shape((8, DH), F32)],
        place,
        onward,
        got,
        carry,
        insides[0],
        specs=[SMEM] + [VMEM] * 3 + [ANY],
    )
    far = across_z(onward, lambda z: z + 3 if z % 2 else z - 3)
    skip = across_z(onward, lambda z: z + 2 if z % 2 else z - 2)
    near = across_z(onward, lambda z: z + 1 if z % 2 else z - 1)
    insides.append(attend(1, onward))
    halves = small(
        halves_kernel,
        [shape((rows // 2, width), BF16)] * 2,
        below,
        above,
        insides[1],
        specs=[ANY] * 3,
        outs=[VMEM] * 2,
        scratch=[dma((2,))],
        mib=4,
    )
    far_weight = along_y(halves[0], 3), along_y(halves[1], 1)
    payload, carry = small(
        pairs_kernel,
        [shape((z_bits * quarter + rows, DH), BF16), shape((8, DH), F32)],
        place,
        onward,
        far,
        skip,
        near,
        carry,
        state,
        halves[0],
        specs=[SMEM] + [VMEM] * 6 + [ANY],
    )
    lefts.append(scaled(1, payload))
    pieces = [payload] + [along_x(payload, d) for d in range(1, NX)]
    rows_out = shape((block // ny, rows), BF16)
    normed = [None] * ny
    normed[1], normed[3], normed[2], states = small(
        finish_kernel,
        [rows_out] * 3 + [shape((heads, (z_bits + PRIOR) * DH, DH), BF16)],
        place,
        carry,
        *insides,
        *lefts,
        pieces[0],
        pieces[1],
        pieces[2],
        pieces[3],
        flops=1 << 28,
    )
    normed[0] = small(
        functools.partial(rows_kernel, (0,)),
        rows_out,
        place,
        *insides,
        *lefts,
        states,
        normed[1],
        specs=[SMEM] + [VMEM] * 5 + [ANY],
        flops=1 << 28,
    )
    normed = [normed[0]] + [along_y(normed[d], d) for d in range(1, ny)]
    columns = 1024 if width % 1024 == 0 else width
    fixed = pl.BlockSpec((2 * CHUNK, rows), lambda i: (0, 0))
    weight_block = pl.BlockSpec((rows, columns), lambda i: (0, i))
    out_block = pl.BlockSpec((CHUNK, columns), lambda i: (0, i))
    half_block = pl.BlockSpec((rows // 2, columns), lambda i: (0, i))
    mine, theirs = pl.pallas_call(
        near_kernel,
        grid=(width // columns,),
        in_specs=[SMEM] + [fixed] * 3 + [weight_block] * 3,
        out_specs=[out_block] * 2,
        out_shape=[shape((CHUNK, width), F32)] * 2,
        scratch_shapes=[pltpu.VMEM((3, 2 * CHUNK, rows), BF16)],
        compiler_params=params(24),
        cost_estimate=pl.CostEstimate(flops=8 << 28, bytes_accessed=5 << 20, transcendentals=0),
    )(place, normed[0], normed[3], normed[1], out_weight, above, below)

    def add_far(side, near, dtype):
        return pl.pallas_call(
            functools.partial(far_kernel, side),
            grid=(width // columns,),
            in_specs=[SMEM, fixed, half_block, half_block, out_block],
            out_specs=out_block,
            out_shape=shape((CHUNK, width), dtype),
            compiler_params=params(24),
            cost_estimate=pl.CostEstimate(flops=1 << 28, bytes_accessed=3 << 20, transcendentals=0),
        )(place, normed[2], *far_weight, near)

    send = add_far(1, theirs, BF16)
    got = lax.ppermute(send, "head", [(i, i ^ 1) for i in range(nh)])
    keep = add_far(0, mine, F32)
    return (keep + got.astype(F32)).astype(BF16)


def solution(mesh):
    placed = (
        P("ctx", None),
        P(None, "head"),
        P(None, "head"),
        P("ctx", "head"),
        P("ctx", None, "head", None, None),
        P("head", None),
    )
    return jax.shard_map(
        shards, mesh=mesh, in_specs=placed, out_specs=P(("ctx", "head"), None), check_vma=False
    )
```

```python
import functools

import jax
import jax.numpy as jnp
from jax import lax
from jax.experimental import pallas as pl
from jax.experimental.pallas import tpu as pltpu
from jax.sharding import PartitionSpec as P

DH = 128
LEVELS = 21
PRIOR = 4
CHUNK = 128
TILE = 256
NX = 4
TAIL = 16
VMEM = pl.BlockSpec(memory_space=pltpu.VMEM)
SMEM = pl.BlockSpec(memory_space=pltpu.SMEM)
F32 = jnp.float32
BF16 = jnp.bfloat16


def params(mib=48):
    return pltpu.CompilerParams(vmem_limit_bytes=mib * 1024 * 1024)


def dot(left, right, contract=((1,), (0,))):
    return lax.dot_general(left, right, (contract, ((), ())), preferred_element_type=F32)


def iota(axis, shape=(CHUNK, CHUNK)):
    return lax.broadcasted_iota(jnp.int32, shape, axis)


def decay_rows(decays):
    rows = iota(0, (TAIL, DH))
    tail = jnp.zeros((TAIL, DH), F32)
    for index, decay in enumerate(decays):
        rest = jnp.broadcast_to(decay, (1, DH))
        for piece in range(3):
            part = rest.astype(BF16).astype(F32)
            tail = jnp.where(rows == index * 3 + piece, part, tail)
            rest = rest - part
    return tail.astype(BF16)


def tail_decays(tail, heads):
    tail = tail.astype(F32)
    return [
        (tail[3 * h : 3 * h + 1] + tail[3 * h + 1 : 3 * h + 2]) + tail[3 * h + 2 : 3 * h + 3]
        for h in range(heads)
    ]


def decays_of(payload, heads):
    return tail_decays(payload[heads * DH : heads * DH + TAIL, :], heads)


def copy_parts(source, target, sems):
    count = sems.shape[0]
    size = target.shape[0] // count
    copies = []
    for i in range(count):
        part = pl.ds(i * size, size)
        copies.append(pltpu.make_async_copy(source.at[part, :], target.at[part, :], sems.at[i]))
    return copies


def keys_kernel(acts_hbm, weight_hbm, kv, query_weight, acts, weight, weight_sem, acts_sem):
    block = acts.shape[0]
    heads = query_weight.shape[1] // DH
    weight_copies = copy_parts(weight_hbm, weight, weight_sem)
    acts_copies = copy_parts(acts_hbm, acts, acts_sem)
    half = len(acts_copies) // 2
    for copy in weight_copies + acts_copies[:half]:
        copy.start()
    for copy in weight_copies:
        copy.wait()
    for copy in acts_copies[half:]:
        copy.start()
    per_tile = len(acts_copies) * TILE // block
    for i in range(block // TILE):
        for copy in acts_copies[i * per_tile : (i + 1) * per_tile]:
            copy.wait()
        token = slice(i * TILE, (i + 1) * TILE)
        for h in range(heads):
            both = dot(acts[token, :], weight[:, h * 3 * DH + DH : (h + 1) * 3 * DH])
            kv[token, h * 2 * DH : (h + 1) * 2 * DH] = both.astype(BF16)
    for h in range(heads):
        query_weight[:, h * DH : (h + 1) * DH] = weight[:, h * 3 * DH : h * 3 * DH + DH]


def states_kernel(place, kv, gate, prior, chunk_states, *payloads):
    x = place[0]
    heads, block = gate.shape
    later = iota(1) > iota(0)
    for h in range(heads):
        rows = slice(h * DH, (h + 1) * DH)
        total = None
        for c in range(block // CHUNK):
            token = slice(c * CHUNK, (c + 1) * CHUNK)
            gates = gate[h : h + 1, token]
            to_end = jnp.exp(jnp.sum(jnp.where(later, gates, 0.0), axis=1, keepdims=True))
            keys = kv[token, 2 * h * DH : (2 * h + 1) * DH].astype(F32)
            values = kv[token, (2 * h + 1) * DH : (2 * h + 2) * DH]
            state = dot((keys * to_end).astype(BF16), values, ((0,), (0,)))
            chunk_states[c, h] = state
            decay = jnp.exp(jnp.sum(gates, axis=1, keepdims=True))
            total = state if total is None else total * decay + state
        for payload in payloads:
            payload[rows, :] = total.astype(BF16)
    tail = decay_rows([jnp.sum(gate[h : h + 1, :], axis=1, keepdims=True) for h in range(heads)])
    start = heads * DH + TAIL
    for d, payload in enumerate(payloads):
        payload[heads * DH : start, :] = tail
        for h in range(heads):
            payload[start + h * DH : start + (h + 1) * DH, :] = prior[x ^ d, h].astype(BF16)


def level_kernel(acts, weight, proj, after, query, level):
    for i in range(acts.shape[0] // TILE):
        rows = slice(i * TILE, (i + 1) * TILE)
        query[rows, :] = dot(acts[rows, :], weight[...]).astype(BF16)
        raw = dot(acts[rows, :], proj[...], ((1,), (1,)))
        value = (jnp.maximum(raw, 0.0) + jnp.log1p(jnp.exp(-jnp.abs(raw)))) * DH ** (-0.5)
        pad = jnp.zeros((TILE, DH - value.shape[1]), F32)
        level[rows, :] = jnp.concatenate([value, pad], axis=1)


def attend_kernel(h, query_rows, kv, level, gate, chunk_states, low_states, after, inside):
    chunks = chunk_states.shape[0]
    low_bits = low_states.shape[0]
    rows, columns = iota(0), iota(1)
    causal = rows >= columns
    differing = jnp.bitwise_xor(rows, columns)
    level_index = jnp.full((CHUNK, CHUNK), h * LEVELS, jnp.int32)
    for bit in range(7):
        level_index = level_index + (differing >= (1 << bit)).astype(jnp.int32)

    totals = [
        jnp.sum(gate[h : h + 1, c * CHUNK : (c + 1) * CHUNK], axis=1, keepdims=True)
        for c in range(chunks)
    ]
    states = {}
    sums = [chunk_states[c, h] for c in range(chunks)]
    for bit in range(3):
        width = 1 << bit
        for low in range(0, chunks, 2 * width):
            state = sums[low // width]
            for c in range(low + width, low + 2 * width):
                states[c, bit] = state.astype(BF16)
                state = state * jnp.exp(totals[c])
            sums[low // width] = state + sums[low // width + 1]
        sums = sums[::2]

    before = jnp.zeros((1, 1), F32)
    for c in range(chunks):
        token = slice(c * CHUNK, (c + 1) * CHUNK)
        level_c = level[token, :]
        gates = gate[h : h + 1, token]
        gate_column = jnp.sum(jnp.where(rows == columns, gates, 0.0), axis=1, keepdims=True)
        column = jnp.sum(jnp.where(causal, gates, 0.0), axis=1, keepdims=True)
        row = jnp.sum(jnp.where(rows <= columns, gate_column, 0.0), axis=0, keepdims=True)
        query = query_rows[token, h * DH : (h + 1) * DH]
        query_f = query.astype(F32)
        scores = dot(query, kv[token, 2 * h * DH : (2 * h + 1) * DH], ((1,), (1,)))
        weights = jnp.take_along_axis(level_c, level_index, axis=1)
        decay = jnp.exp(jnp.where(causal, column - row, -1e30))
        lhs = [(weights * decay * scores).astype(BF16)]
        rhs = [kv[token, (2 * h + 1) * DH : (2 * h + 2) * DH]]
        chunk_level = level_c * jnp.exp(column)
        for bit in range(3):
            if (c, bit) in states:
                where = h * LEVELS + 8 + bit
                lhs.append((chunk_level[:, where : where + 1] * query_f).astype(BF16))
                rhs.append(states[c, bit])
        block_level = level_c * jnp.exp(column + before)
        for n in range(low_bits):
            where = h * LEVELS + 11 + n
            lhs.append((block_level[:, where : where + 1] * query_f).astype(BF16))
            rhs.append(low_states[n, h])
        inside[token, :] = dot(jnp.concatenate(lhs, axis=1), jnp.concatenate(rhs, axis=0))
        before = before + totals[c]


def scale_kernel(h, query_rows, level, gate, after, left):
    causal = iota(0) >= iota(1)
    before = jnp.zeros((1, 1), F32)
    for c in range(left.shape[0] // CHUNK):
        token = slice(c * CHUNK, (c + 1) * CHUNK)
        gates = gate[h : h + 1, token]
        column = jnp.sum(jnp.where(causal, gates, 0.0), axis=1, keepdims=True)
        block_level = level[token, :] * jnp.exp(column + before)
        query_f = query_rows[token, h * DH : (h + 1) * DH].astype(F32)
        for n in range(left.shape[1] // DH):
            where = h * LEVELS + 13 + n
            left[token, n * DH : (n + 1) * DH] = (
                block_level[:, where : where + 1] * query_f
            ).astype(BF16)
        before = before + jnp.sum(gates, axis=1, keepdims=True)


def within_kernel(place, own, two, one, three, after, states, onward, carry):
    pieces = (own, one, two, three)
    x = place[0]
    heads = states.shape[1]
    start = heads * DH + TAIL
    quarter = heads * DH // NX
    owner = [x ^ d for d in range(NX)]
    decays = [decays_of(piece, heads) for piece in pieces]
    group_decay = []
    carry[...] = jnp.zeros_like(carry)
    for h in range(heads):
        rows = slice(h * DH, (h + 1) * DH)
        bits = [jnp.zeros((DH, DH), F32) for _ in range(2)]
        before = jnp.zeros((1, DH), F32)
        whole = jnp.zeros((1, DH), F32)
        for d in range(NX):
            whole = whole + decays[d][h]
            before = before + jnp.where(owner[d] < x, decays[d][h], 0.0)
            if d == 0:
                continue
            piece = pieces[d][rows, :].astype(F32)
            to_here = jnp.zeros((1, DH), F32)
            for e in range(1, NX):
                after_it = (owner[e] > owner[d]) & (owner[e] < x)
                to_here = to_here + jnp.where(after_it, decays[e][h], 0.0)
            scale = jnp.where(owner[d] < x, jnp.exp(to_here), 0.0)
            for bit in range(2):
                used = (
                    (((x >> bit) & 1) == 1)
                    & (((owner[d] >> bit) & 1) == 0)
                    & ((x >> (bit + 1)) == (owner[d] >> (bit + 1)))
                )
                bits[bit] = bits[bit] + piece * jnp.where(used, scale, 0.0)
        for bit in range(2):
            states[bit, h] = bits[bit].astype(BF16)
        carry[h : h + 1, :] = before
        group_decay.append(whole)
    mine = pl.ds(pl.multiple_of(x * quarter, quarter), quarter)
    group = jnp.zeros((quarter, DH), F32)
    for d in range(NX):
        to_end = jnp.zeros((1, DH), F32)
        for e in range(NX):
            decay = jnp.where(x < NX // 2, decays[e][0], decays[e][1])
            to_end = to_end + jnp.where(owner[e] > owner[d], decay, 0.0)
        group = group + pieces[d][mine, :].astype(F32) * jnp.exp(to_end)
    onward[:quarter, :] = group.astype(BF16)
    onward[quarter : quarter + TAIL, :] = decay_rows(group_decay)
    prior = own[start:, :].astype(F32)
    for piece in pieces[1:]:
        prior = prior + piece[start:, :].astype(F32)
    onward[quarter + TAIL :, :] = prior.astype(BF16)


def halves_kernel(below, above, after, first, second, sems):
    size = first.shape[0]
    copies = [
        pltpu.make_async_copy(below.at[pl.ds(0, size), :], first, sems.at[0]),
        pltpu.make_async_copy(above.at[pl.ds(size, size), :], second, sems.at[1]),
    ]
    for copy in copies:
        copy.start()
    for copy in copies:
        copy.wait()


def pair_kernel(place, own, got, carry_in, after, state_out, onward, carry):
    x, z = place[0], place[1]
    heads = 2
    quarter = heads * DH // NX
    upper = (z & 1) == 1
    decay_own = tail_decays(own[quarter : quarter + TAIL, :], heads)
    decay_got = tail_decays(got[quarter : quarter + TAIL, :], heads)
    carry[...] = jnp.zeros_like(carry)
    for h in range(heads):
        before = carry_in[h : h + 1, :]
        carry[2 + h : 3 + h, :] = before
        carry[h : h + 1, :] = before + jnp.where(upper, decay_got[h], 0.0)
    state_out[...] = jnp.where(upper, got[:quarter, :].astype(F32), 0.0).astype(BF16)
    first = x < NX // 2
    mine = jnp.where(first, decay_own[0], decay_own[1])
    theirs = jnp.where(first, decay_got[0], decay_got[1])
    scale_own = jnp.where(upper, 1.0, jnp.exp(theirs))
    scale_got = jnp.where(upper, jnp.exp(mine), 1.0)
    total = own[:quarter, :].astype(F32) * scale_own + got[:quarter, :].astype(F32) * scale_got
    onward[:quarter, :] = total.astype(BF16)
    onward[quarter : quarter + TAIL, :] = decay_rows(
        [decay_own[h] + decay_got[h] for h in range(heads)]
    )
    prior = own[quarter + TAIL :, :].astype(F32) + got[quarter + TAIL :, :].astype(F32)
    onward[quarter + TAIL :, :] = prior.astype(BF16)


def pairs_kernel(place, own, far, skip, near, carry_in, low_state, after, payload, carry):
    x, z = place[0], place[1]
    heads = 2
    quarter = heads * DH // NX
    pair = z >> 1
    odd = (z & 1) == 1
    prior = slice(quarter + TAIL, own.shape[0])
    total = own[prior, :].astype(F32) + near[prior, :].astype(F32)
    total = total + skip[prior, :].astype(F32) + far[prior, :].astype(F32)

    def pick(flag, left, right):
        return jnp.where(flag, left, right)

    tail = slice(quarter, quarter + TAIL)
    tail_near, tail_skip = near[tail, :].astype(F32), skip[tail, :].astype(F32)
    decay_next = tail_decays(pick(odd, tail_near, tail_skip), heads)
    decay_prev = tail_decays(pick(odd, tail_skip, tail_near), heads)
    decay_far = tail_decays(far[tail, :], heads)
    carry[...] = carry_in[...]
    for h in range(heads):
        before = carry_in[h : h + 1, :]
        carry[4 + h : 5 + h, :] = before
        carry[6 + h : 7 + h, :] = before + pick(pair == 3, decay_prev[h], 0.0)
        offset = before + pick(pair >= 1, decay_prev[h], 0.0) + pick(pair >= 2, decay_far[h], 0.0)
        carry[h : h + 1, :] = offset + pick(pair == 3, decay_next[h], 0.0)
    state_near, state_skip = near[:quarter, :].astype(F32), skip[:quarter, :].astype(F32)
    state_next = pick(odd, state_near, state_skip)
    state_prev = pick(odd, state_skip, state_near)
    state_far = far[:quarter, :].astype(F32)
    first = x < NX // 2
    decay_one = pick(
        pair == 2,
        pick(first, decay_prev[0], decay_prev[1]),
        pick(first, decay_far[0], decay_far[1]),
    )
    zero_state = pick(pair == 2, state_far, state_next)
    one_state = pick(pair == 2, state_prev, state_far)
    high = pick(pair >= 2, zero_state * jnp.exp(decay_one) + one_state, 0.0)
    payload[:quarter, :] = low_state[...]
    payload[quarter : 2 * quarter, :] = pick((pair & 1) == 1, state_prev, 0.0).astype(BF16)
    payload[2 * quarter : 3 * quarter, :] = high.astype(BF16)
    payload[3 * quarter :, :] = total.astype(BF16)


def finish_kernel(place, carry, *refs):
    heads = 2
    insides, lefts, refs = refs[:heads], refs[heads : 2 * heads], refs[2 * heads :]
    own, one, two, three = refs[:NX]
    pieces, outs, states = (own, one, two, three), refs[NX:-1], refs[-1]
    z_bits = lefts[0].shape[1] // DH - PRIOR
    x = place[0]
    quarter = heads * DH // NX
    offsets = [jnp.exp(carry[h : h + 1, :]) for h in range(heads)]
    for d in range(NX):
        owner = x ^ d
        first = owner < NX // 2
        for bit in range(z_bits):
            before = jnp.where(first, carry[2 + 2 * bit : 3 + 2 * bit, :], carry[3 + 2 * bit : 4 + 2 * bit, :])
            piece = pieces[d][bit * quarter : (bit + 1) * quarter, :].astype(F32) * jnp.exp(before)
            where = bit * DH + lax.rem(owner, 2) * quarter
            states[owner // 2, pl.ds(pl.multiple_of(where, quarter), quarter), :] = piece.astype(BF16)
        for h in range(heads):
            rows = slice(z_bits * quarter + h * DH, z_bits * quarter + (h + 1) * DH)
            where = pl.multiple_of((z_bits + owner) * DH, DH)
            piece = pieces[d][rows, :].astype(F32) * offsets[h]
            states[h, pl.ds(where, DH), :] = piece.astype(BF16)
    rows_kernel((1, 3, 2), place, *insides, *lefts, states, *outs)


def rows_kernel(distances, place, *refs):
    heads = 2
    insides, lefts = refs[:heads], refs[heads : 2 * heads]
    states, outs = refs[2 * heads], refs[-len(distances) :]
    for d, out in zip(distances, outs):
        chip = place[2] ^ d
        token = pl.ds(pl.multiple_of(chip * TILE, TILE), TILE)
        for h in range(heads):
            u = insides[h][token, :] + dot(lefts[h][token, :], states[h])
            normed = u * lax.rsqrt(jnp.mean(u * u, axis=1, keepdims=True) + 1e-06)
            out[:, h * DH : (h + 1) * DH] = normed.astype(BF16)


def near_kernel(place, *refs):
    refs, (mine, theirs, rows) = refs[:-3], refs[-3:]
    pieces, weights = refs[: len(refs) // 2], refs[len(refs) // 2 :]

    @pl.when(pl.program_id(0) == 0)
    def _():
        for d, piece in enumerate(pieces):
            for side in range(2):
                where = pl.multiple_of((place[3] ^ side) * CHUNK, CHUNK)
                rows[d, side * CHUNK : (side + 1) * CHUNK, :] = piece[pl.ds(where, CHUNK), :]

    total = dot(rows[0], weights[0][...])
    for d in range(1, len(pieces)):
        total = total + dot(rows[d], weights[d][...])
    mine[...] = total[:CHUNK]
    theirs[...] = total[CHUNK:]


def far_kernel(side, place, piece, first, second, near, out):
    weight = jnp.concatenate([first[...], second[...]], axis=0)
    where = pl.multiple_of((place[3] ^ side) * CHUNK, CHUNK)
    total = near[...] + dot(piece[pl.ds(where, CHUNK), :], weight)
    out[...] = total.astype(out.dtype)


def last_kernel(keep, *refs):
    swapped, out = refs[:-1], refs[-1]
    for i, got in enumerate(swapped):

        @pl.when(pl.program_id(0) == i)
        def _(got=got):
            out[...] = (keep[...] + got[...].astype(F32)).astype(BF16)


ANY = pl.BlockSpec(memory_space=pl.ANY)
HBM = pl.BlockSpec(memory_space=pltpu.HBM)


def small(kernel, shapes, *operands, specs=None, outs=None, scratch=(), flops=0, mib=24):
    return pl.pallas_call(
        kernel,
        out_shape=shapes,
        in_specs=specs or [SMEM if o.dtype == jnp.int32 else VMEM for o in operands],
        out_specs=outs or jax.tree.map(lambda _: VMEM, shapes),
        scratch_shapes=list(scratch),
        compiler_params=params(mib),
        cost_estimate=pl.CostEstimate(flops=flops, bytes_accessed=1 << 20, transcendentals=0),
    )(*operands)


def shards(activations, qkv_weight, level_proj, log_gate, prior_parts, out_weight):
    block, width = activations.shape
    heads = log_gate.shape[1]
    nz = lax.axis_size("ctx") // NX
    nh = lax.axis_size("head")
    ny = nh // 2
    z_bits = nz.bit_length() - 1
    chunks = block // CHUNK
    rows = heads * DH
    quarter = rows // NX
    shape = jax.ShapeDtypeStruct
    ctx = lax.axis_index("ctx").astype(jnp.int32)
    head = lax.axis_index("head").astype(jnp.int32)
    place = jnp.stack([ctx % NX, ctx // NX, head // 2, head % 2])

    def along_x(array, d):
        return lax.ppermute(
            array, "ctx", [(z * NX + x, z * NX + (x ^ d)) for z in range(nz) for x in range(NX)]
        )

    def across_z(array, target):
        return lax.ppermute(
            array, "ctx", [(z * NX + x, target(z) % nz * NX + x) for z in range(nz) for x in range(NX)]
        )

    def along_y(array, d):
        return lax.ppermute(
            array, "head", [(y * 2 + c, (y ^ d) * 2 + c) for y in range(ny) for c in range(2)]
        )

    below, above = along_y(out_weight, 1), along_y(out_weight, 3)
    gate = log_gate.T
    sent = shape((rows + TAIL + rows, DH), BF16)
    dma = pltpu.SemaphoreType.DMA
    kv, query_weight = small(
        keys_kernel,
        [shape((block, 2 * rows), BF16), shape((width, rows), BF16)],
        activations,
        qkv_weight,
        specs=[HBM] * 2,
        scratch=[
            pltpu.VMEM(activations.shape, BF16),
            pltpu.VMEM(qkv_weight.shape, BF16),
            dma((8,)),
            dma((8,)),
        ],
        flops=4 * block * width * rows,
        mib=50,
    )
    chunk_states, *payloads = small(
        states_kernel,
        [shape((chunks, heads, DH, DH), F32)] + [sent] * NX,
        place,
        kv,
        gate,
        prior_parts[0],
    )
    pieces = [payloads[0]] + [along_x(payloads[d], d) for d in range(1, NX)]

    query, level = small(
        level_kernel,
        [shape((block, rows), BF16), shape((block, DH), F32)],
        activations,
        query_weight,
        level_proj.T,
        payloads[0],
        specs=[VMEM] * 3 + [ANY],
        flops=4 * block * width * rows,
        mib=24,
    )

    def scaled(h, after):
        return small(
            functools.partial(scale_kernel, h),
            shape((block, (z_bits + PRIOR) * DH), BF16),
            query,
            level,
            gate,
            after,
            specs=[VMEM] * 3 + [ANY],
            flops=1 << 30,
        )

    lefts = [scaled(0, payloads[0])]
    low_states, onward, carry = small(
        within_kernel,
        [
            shape((2, heads, DH, DH), BF16),
            shape((quarter + TAIL + rows, DH), BF16),
            shape((8, DH), F32),
        ],
        place,
        pieces[0],
        pieces[2],
        pieces[1],
        pieces[3],
        lefts[0],
        specs=[SMEM] + [VMEM] * NX + [ANY],
    )

    def attend(h, after):
        return small(
            functools.partial(attend_kernel, h),
            shape((block, DH), F32),
            query,
            kv,
            level,
            gate,
            chunk_states,
            low_states,
            after,
            specs=[VMEM] * 6 + [ANY],
            flops=1 << 30,
        )

    got = across_z(onward, lambda z: z ^ 1)
    insides = [attend(0, onward)]
    state, onward, carry = small(
        pair_kernel,
        [shape((quarter, DH), BF16), shape(onward.shape, BF16), shape((8, DH), F32)],
        place,
        onward,
        got,
        carry,
        insides[0],
        specs=[SMEM] + [VMEM] * 3 + [ANY],
    )
    far = across_z(onward, lambda z: z + 3 if z % 2 else z - 3)
    skip = across_z(onward, lambda z: z + 2 if z % 2 else z - 2)
    near = across_z(onward, lambda z: z + 1 if z % 2 else z - 1)
    insides.append(attend(1, onward))
    halves = small(
        halves_kernel,
        [shape((rows // 2, width), BF16)] * 2,
        below,
        above,
        insides[1],
        specs=[ANY] * 3,
        outs=[VMEM] * 2,
        scratch=[dma((2,))],
        mib=4,
    )
    far_weight = along_y(halves[0], 3), along_y(halves[1], 1)
    payload, carry = small(
        pairs_kernel,
        [shape((z_bits * quarter + rows, DH), BF16), shape((8, DH), F32)],
        place,
        onward,
        far,
        skip,
        near,
        carry,
        state,
        halves[0],
        specs=[SMEM] + [VMEM] * 6 + [ANY],
    )
    lefts.append(scaled(1, payload))
    pieces = [payload] + [along_x(payload, d) for d in range(1, NX)]
    rows_out = shape((block // ny, rows), BF16)
    normed = [None] * ny
    normed[1], normed[3], normed[2], states = small(
        finish_kernel,
        [rows_out] * 3 + [shape((heads, (z_bits + PRIOR) * DH, DH), BF16)],
        place,
        carry,
        *insides,
        *lefts,
        pieces[0],
        pieces[1],
        pieces[2],
        pieces[3],
        flops=1 << 28,
    )
    normed[0] = small(
        functools.partial(rows_kernel, (0,)),
        rows_out,
        place,
        *insides,
        *lefts,
        states,
        normed[1],
        specs=[SMEM] + [VMEM] * 5 + [ANY],
        flops=1 << 28,
    )
    normed = [normed[0]] + [along_y(normed[d], d) for d in range(1, ny)]
    columns = 1024 if width % 1024 == 0 else width
    fixed = pl.BlockSpec((2 * CHUNK, rows), lambda i: (0, 0))
    weight_block = pl.BlockSpec((rows, columns), lambda i: (0, i))
    out_block = pl.BlockSpec((CHUNK, columns), lambda i: (0, i))
    half_block = pl.BlockSpec((rows // 2, columns), lambda i: (0, i))
    mine, theirs = pl.pallas_call(
        near_kernel,
        grid=(width // columns,),
        in_specs=[SMEM] + [fixed] * 3 + [weight_block] * 3,
        out_specs=[out_block] * 2,
        out_shape=[shape((CHUNK, width), F32)] * 2,
        scratch_shapes=[pltpu.VMEM((3, 2 * CHUNK, rows), BF16)],
        compiler_params=params(24),
        cost_estimate=pl.CostEstimate(flops=8 << 28, bytes_accessed=5 << 20, transcendentals=0),
    )(place, normed[0], normed[3], normed[1], out_weight, above, below)

    def add_far(side, near, dtype, first, count):
        shift = lambda block: pl.BlockSpec(block.block_shape, lambda i: (0, first + i))
        return pl.pallas_call(
            functools.partial(far_kernel, side),
            grid=(count,),
            in_specs=[SMEM, fixed, shift(half_block), shift(half_block), shift(out_block)],
            out_specs=out_block,
            out_shape=shape((CHUNK, count * columns), dtype),
            compiler_params=params(24),
            cost_estimate=pl.CostEstimate(flops=1 << 28, bytes_accessed=3 << 20, transcendentals=0),
        )(place, normed[2], *far_weight, near)

    count = width // columns
    swapped = [
        lax.ppermute(add_far(1, theirs, BF16, i, 1), "head", [(i, i ^ 1) for i in range(nh)])
        for i in range(count)
    ]
    keep = add_far(0, mine, F32, 0, count)
    return pl.pallas_call(
        last_kernel,
        grid=(count,),
        in_specs=[out_block] + [pl.BlockSpec((CHUNK, columns), lambda i: (0, 0))] * count,
        out_specs=out_block,
        out_shape=shape((CHUNK, width), BF16),
        compiler_params=params(24),
    )(keep, *swapped)


def solution(mesh):
    placed = (
        P("ctx", None),
        P(None, "head"),
        P(None, "head"),
        P("ctx", "head"),
        P("ctx", None, "head", None, None),
        P("head", None),
    )
    return jax.shard_map(
        shards, mesh=mesh, in_specs=placed, out_specs=P(("ctx", "head"), None), check_vma=False
    )
```

```python
import functools

import jax
import jax.numpy as jnp
from jax import lax
from jax.experimental import pallas as pl
from jax.experimental.pallas import tpu as pltpu
from jax.sharding import PartitionSpec as P

DH = 128
LEVELS = 21
PRIOR = 4
CHUNK = 128
TILE = 256
NX = 4
TAIL = 16
VMEM = pl.BlockSpec(memory_space=pltpu.VMEM)
SMEM = pl.BlockSpec(memory_space=pltpu.SMEM)
F32 = jnp.float32
BF16 = jnp.bfloat16


def params(mib=48):
    return pltpu.CompilerParams(vmem_limit_bytes=mib * 1024 * 1024)


def dot(left, right, contract=((1,), (0,))):
    return lax.dot_general(left, right, (contract, ((), ())), preferred_element_type=F32)


def iota(axis, shape=(CHUNK, CHUNK)):
    return lax.broadcasted_iota(jnp.int32, shape, axis)


def decay_rows(decays):
    rows = iota(0, (TAIL, DH))
    tail = jnp.zeros((TAIL, DH), F32)
    for index, decay in enumerate(decays):
        rest = jnp.broadcast_to(decay, (1, DH))
        for piece in range(3):
            part = rest.astype(BF16).astype(F32)
            tail = jnp.where(rows == index * 3 + piece, part, tail)
            rest = rest - part
    return tail.astype(BF16)


def tail_decays(tail, heads):
    tail = tail.astype(F32)
    return [
        (tail[3 * h : 3 * h + 1] + tail[3 * h + 1 : 3 * h + 2]) + tail[3 * h + 2 : 3 * h + 3]
        for h in range(heads)
    ]


def decays_of(payload, heads):
    return tail_decays(payload[heads * DH : heads * DH + TAIL, :], heads)


def copy_parts(source, target, sems):
    count = sems.shape[0]
    size = target.shape[0] // count
    copies = []
    for i in range(count):
        part = pl.ds(i * size, size)
        copies.append(pltpu.make_async_copy(source.at[part, :], target.at[part, :], sems.at[i]))
    return copies


def keys_kernel(acts_hbm, weight_hbm, kv, query_weight, acts, weight, weight_sem, acts_sem):
    block = acts.shape[0]
    heads = query_weight.shape[1] // DH
    weight_copies = copy_parts(weight_hbm, weight, weight_sem)
    acts_copies = copy_parts(acts_hbm, acts, acts_sem)
    half = len(acts_copies) // 2
    for copy in weight_copies + acts_copies[:half]:
        copy.start()
    for copy in weight_copies:
        copy.wait()
    for copy in acts_copies[half:]:
        copy.start()
    per_tile = len(acts_copies) * TILE // block
    for i in range(block // TILE):
        for copy in acts_copies[i * per_tile : (i + 1) * per_tile]:
            copy.wait()
        token = slice(i * TILE, (i + 1) * TILE)
        for h in range(heads):
            both = dot(acts[token, :], weight[:, h * 3 * DH + DH : (h + 1) * 3 * DH])
            kv[token, h * 2 * DH : (h + 1) * 2 * DH] = both.astype(BF16)
    for h in range(heads):
        query_weight[:, h * DH : (h + 1) * DH] = weight[:, h * 3 * DH : h * 3 * DH + DH]


def states_kernel(place, kv, gate, prior, chunk_states, *payloads):
    x = place[0]
    heads, block = gate.shape
    later = iota(1) > iota(0)
    for h in range(heads):
        rows = slice(h * DH, (h + 1) * DH)
        total = None
        for c in range(block // CHUNK):
            token = slice(c * CHUNK, (c + 1) * CHUNK)
            gates = gate[h : h + 1, token]
            to_end = jnp.exp(jnp.sum(jnp.where(later, gates, 0.0), axis=1, keepdims=True))
            keys = kv[token, 2 * h * DH : (2 * h + 1) * DH].astype(F32)
            values = kv[token, (2 * h + 1) * DH : (2 * h + 2) * DH]
            state = dot((keys * to_end).astype(BF16), values, ((0,), (0,)))
            chunk_states[c, h] = state
            decay = jnp.exp(jnp.sum(gates, axis=1, keepdims=True))
            total = state if total is None else total * decay + state
        for payload in payloads:
            payload[rows, :] = total.astype(BF16)
    tail = decay_rows([jnp.sum(gate[h : h + 1, :], axis=1, keepdims=True) for h in range(heads)])
    start = heads * DH + TAIL
    for d, payload in enumerate(payloads):
        payload[heads * DH : start, :] = tail
        for h in range(heads):
            payload[start + h * DH : start + (h + 1) * DH, :] = prior[x ^ d, h].astype(BF16)


def level_kernel(acts, weight, proj, after, query, level):
    for i in range(acts.shape[0] // TILE):
        rows = slice(i * TILE, (i + 1) * TILE)
        query[rows, :] = dot(acts[rows, :], weight[...]).astype(BF16)
        raw = dot(acts[rows, :], proj[...], ((1,), (1,)))
        value = (jnp.maximum(raw, 0.0) + jnp.log1p(jnp.exp(-jnp.abs(raw)))) * DH ** (-0.5)
        pad = jnp.zeros((TILE, DH - value.shape[1]), F32)
        level[rows, :] = jnp.concatenate([value, pad], axis=1)


def attend_kernel(h, query_rows, kv, level, gate, chunk_states, low_states, after, inside):
    chunks = chunk_states.shape[0]
    low_bits = low_states.shape[0]
    rows, columns = iota(0), iota(1)
    causal = rows >= columns
    differing = jnp.bitwise_xor(rows, columns)
    level_index = jnp.full((CHUNK, CHUNK), h * LEVELS, jnp.int32)
    for bit in range(7):
        level_index = level_index + (differing >= (1 << bit)).astype(jnp.int32)

    totals = [
        jnp.sum(gate[h : h + 1, c * CHUNK : (c + 1) * CHUNK], axis=1, keepdims=True)
        for c in range(chunks)
    ]
    states = {}
    sums = [chunk_states[c, h] for c in range(chunks)]
    for bit in range(3):
        width = 1 << bit
        for low in range(0, chunks, 2 * width):
            state = sums[low // width]
            for c in range(low + width, low + 2 * width):
                states[c, bit] = state.astype(BF16)
                state = state * jnp.exp(totals[c])
            sums[low // width] = state + sums[low // width + 1]
        sums = sums[::2]

    before = jnp.zeros((1, 1), F32)
    for c in range(chunks):
        token = slice(c * CHUNK, (c + 1) * CHUNK)
        level_c = level[token, :]
        gates = gate[h : h + 1, token]
        gate_column = jnp.sum(jnp.where(rows == columns, gates, 0.0), axis=1, keepdims=True)
        column = jnp.sum(jnp.where(causal, gates, 0.0), axis=1, keepdims=True)
        row = jnp.sum(jnp.where(rows <= columns, gate_column, 0.0), axis=0, keepdims=True)
        query = query_rows[token, h * DH : (h + 1) * DH]
        query_f = query.astype(F32)
        scores = dot(query, kv[token, 2 * h * DH : (2 * h + 1) * DH], ((1,), (1,)))
        weights = jnp.take_along_axis(level_c, level_index, axis=1)
        decay = jnp.exp(jnp.where(causal, column - row, -1e30))
        lhs = [(weights * decay * scores).astype(BF16)]
        rhs = [kv[token, (2 * h + 1) * DH : (2 * h + 2) * DH]]
        chunk_level = level_c * jnp.exp(column)
        for bit in range(3):
            if (c, bit) in states:
                where = h * LEVELS + 8 + bit
                lhs.append((chunk_level[:, where : where + 1] * query_f).astype(BF16))
                rhs.append(states[c, bit])
        block_level = level_c * jnp.exp(column + before)
        for n in range(low_bits):
            where = h * LEVELS + 11 + n
            lhs.append((block_level[:, where : where + 1] * query_f).astype(BF16))
            rhs.append(low_states[n, h])
        inside[token, :] = dot(jnp.concatenate(lhs, axis=1), jnp.concatenate(rhs, axis=0))
        before = before + totals[c]


def scale_kernel(h, query_rows, level, gate, after, left):
    causal = iota(0) >= iota(1)
    before = jnp.zeros((1, 1), F32)
    for c in range(left.shape[0] // CHUNK):
        token = slice(c * CHUNK, (c + 1) * CHUNK)
        gates = gate[h : h + 1, token]
        column = jnp.sum(jnp.where(causal, gates, 0.0), axis=1, keepdims=True)
        block_level = level[token, :] * jnp.exp(column + before)
        query_f = query_rows[token, h * DH : (h + 1) * DH].astype(F32)
        for n in range(left.shape[1] // DH):
            where = h * LEVELS + 13 + n
            left[token, n * DH : (n + 1) * DH] = (
                block_level[:, where : where + 1] * query_f
            ).astype(BF16)
        before = before + jnp.sum(gates, axis=1, keepdims=True)


def within_kernel(place, own, two, three, one, after, states, onward, carry):
    pieces = (own, one, two, three)
    x = place[0]
    heads = states.shape[1]
    start = heads * DH + TAIL
    quarter = heads * DH // NX
    owner = [x ^ d for d in range(NX)]
    decays = [decays_of(piece, heads) for piece in pieces]
    group_decay = []
    carry[...] = jnp.zeros_like(carry)
    for h in range(heads):
        rows = slice(h * DH, (h + 1) * DH)
        bits = [jnp.zeros((DH, DH), F32) for _ in range(2)]
        before = jnp.zeros((1, DH), F32)
        whole = jnp.zeros((1, DH), F32)
        for d in range(NX):
            whole = whole + decays[d][h]
            before = before + jnp.where(owner[d] < x, decays[d][h], 0.0)
            if d == 0:
                continue
            piece = pieces[d][rows, :].astype(F32)
            to_here = jnp.zeros((1, DH), F32)
            for e in range(1, NX):
                after_it = (owner[e] > owner[d]) & (owner[e] < x)
                to_here = to_here + jnp.where(after_it, decays[e][h], 0.0)
            scale = jnp.where(owner[d] < x, jnp.exp(to_here), 0.0)
            for bit in range(2):
                used = (
                    (((x >> bit) & 1) == 1)
                    & (((owner[d] >> bit) & 1) == 0)
                    & ((x >> (bit + 1)) == (owner[d] >> (bit + 1)))
                )
                bits[bit] = bits[bit] + piece * jnp.where(used, scale, 0.0)
        for bit in range(2):
            states[bit, h] = bits[bit].astype(BF16)
        carry[h : h + 1, :] = before
        group_decay.append(whole)
    mine = pl.ds(pl.multiple_of(x * quarter, quarter), quarter)
    group = jnp.zeros((quarter, DH), F32)
    for d in range(NX):
        to_end = jnp.zeros((1, DH), F32)
        for e in range(NX):
            decay = jnp.where(x < NX // 2, decays[e][0], decays[e][1])
            to_end = to_end + jnp.where(owner[e] > owner[d], decay, 0.0)
        group = group + pieces[d][mine, :].astype(F32) * jnp.exp(to_end)
    onward[:quarter, :] = group.astype(BF16)
    onward[quarter : quarter + TAIL, :] = decay_rows(group_decay)
    prior = own[start:, :].astype(F32)
    for piece in pieces[1:]:
        prior = prior + piece[start:, :].astype(F32)
    onward[quarter + TAIL :, :] = prior.astype(BF16)


def halves_kernel(below, above, after, first, second, sems):
    size = first.shape[0]
    copies = [
        pltpu.make_async_copy(below.at[pl.ds(0, size), :], first, sems.at[0]),
        pltpu.make_async_copy(above.at[pl.ds(size, size), :], second, sems.at[1]),
    ]
    for copy in copies:
        copy.start()
    for copy in copies:
        copy.wait()


def pair_kernel(place, own, got, carry_in, after, state_out, onward, carry):
    x, z = place[0], place[1]
    heads = 2
    quarter = heads * DH // NX
    upper = (z & 1) == 1
    decay_own = tail_decays(own[quarter : quarter + TAIL, :], heads)
    decay_got = tail_decays(got[quarter : quarter + TAIL, :], heads)
    carry[...] = jnp.zeros_like(carry)
    for h in range(heads):
        before = carry_in[h : h + 1, :]
        carry[2 + h : 3 + h, :] = before
        carry[h : h + 1, :] = before + jnp.where(upper, decay_got[h], 0.0)
    state_out[...] = jnp.where(upper, got[:quarter, :].astype(F32), 0.0).astype(BF16)
    first = x < NX // 2
    mine = jnp.where(first, decay_own[0], decay_own[1])
    theirs = jnp.where(first, decay_got[0], decay_got[1])
    scale_own = jnp.where(upper, 1.0, jnp.exp(theirs))
    scale_got = jnp.where(upper, jnp.exp(mine), 1.0)
    total = own[:quarter, :].astype(F32) * scale_own + got[:quarter, :].astype(F32) * scale_got
    onward[:quarter, :] = total.astype(BF16)
    onward[quarter : quarter + TAIL, :] = decay_rows(
        [decay_own[h] + decay_got[h] for h in range(heads)]
    )
    prior = own[quarter + TAIL :, :].astype(F32) + got[quarter + TAIL :, :].astype(F32)
    onward[quarter + TAIL :, :] = prior.astype(BF16)


def pairs_kernel(place, own, far, skip, near, carry_in, low_state, after, payload, carry):
    x, z = place[0], place[1]
    heads = 2
    quarter = heads * DH // NX
    pair = z >> 1
    odd = (z & 1) == 1
    prior = slice(quarter + TAIL, own.shape[0])
    total = own[prior, :].astype(F32) + near[prior, :].astype(F32)
    total = total + skip[prior, :].astype(F32) + far[prior, :].astype(F32)

    def pick(flag, left, right):
        return jnp.where(flag, left, right)

    tail = slice(quarter, quarter + TAIL)
    tail_near, tail_skip = near[tail, :].astype(F32), skip[tail, :].astype(F32)
    decay_next = tail_decays(pick(odd, tail_near, tail_skip), heads)
    decay_prev = tail_decays(pick(odd, tail_skip, tail_near), heads)
    decay_far = tail_decays(far[tail, :], heads)
    carry[...] = carry_in[...]
    for h in range(heads):
        before = carry_in[h : h + 1, :]
        carry[4 + h : 5 + h, :] = before
        carry[6 + h : 7 + h, :] = before + pick(pair == 3, decay_prev[h], 0.0)
        offset = before + pick(pair >= 1, decay_prev[h], 0.0) + pick(pair >= 2, decay_far[h], 0.0)
        carry[h : h + 1, :] = offset + pick(pair == 3, decay_next[h], 0.0)
    state_near, state_skip = near[:quarter, :].astype(F32), skip[:quarter, :].astype(F32)
    state_next = pick(odd, state_near, state_skip)
    state_prev = pick(odd, state_skip, state_near)
    state_far = far[:quarter, :].astype(F32)
    first = x < NX // 2
    decay_one = pick(
        pair == 2,
        pick(first, decay_prev[0], decay_prev[1]),
        pick(first, decay_far[0], decay_far[1]),
    )
    zero_state = pick(pair == 2, state_far, state_next)
    one_state = pick(pair == 2, state_prev, state_far)
    high = pick(pair >= 2, zero_state * jnp.exp(decay_one) + one_state, 0.0)
    payload[:quarter, :] = low_state[...]
    payload[quarter : 2 * quarter, :] = pick((pair & 1) == 1, state_prev, 0.0).astype(BF16)
    payload[2 * quarter : 3 * quarter, :] = high.astype(BF16)
    payload[3 * quarter :, :] = total.astype(BF16)


def finish_kernel(place, carry, *refs):
    heads = 2
    insides, lefts, refs = refs[:heads], refs[heads : 2 * heads], refs[2 * heads :]
    own, one, two, three = refs[:NX]
    pieces, outs, states = (own, one, two, three), refs[NX:-1], refs[-1]
    z_bits = lefts[0].shape[1] // DH - PRIOR
    x = place[0]
    quarter = heads * DH // NX
    offsets = [jnp.exp(carry[h : h + 1, :]) for h in range(heads)]
    for d in range(NX):
        owner = x ^ d
        first = owner < NX // 2
        for bit in range(z_bits):
            before = jnp.where(first, carry[2 + 2 * bit : 3 + 2 * bit, :], carry[3 + 2 * bit : 4 + 2 * bit, :])
            piece = pieces[d][bit * quarter : (bit + 1) * quarter, :].astype(F32) * jnp.exp(before)
            where = bit * DH + lax.rem(owner, 2) * quarter
            states[owner // 2, pl.ds(pl.multiple_of(where, quarter), quarter), :] = piece.astype(BF16)
        for h in range(heads):
            rows = slice(z_bits * quarter + h * DH, z_bits * quarter + (h + 1) * DH)
            where = pl.multiple_of((z_bits + owner) * DH, DH)
            piece = pieces[d][rows, :].astype(F32) * offsets[h]
            states[h, pl.ds(where, DH), :] = piece.astype(BF16)
    rows_kernel((1, 3, 2), place, *insides, *lefts, states, *outs)


def rows_kernel(distances, place, *refs):
    heads = 2
    insides, lefts = refs[:heads], refs[heads : 2 * heads]
    states, outs = refs[2 * heads], refs[-len(distances) :]
    for d, out in zip(distances, outs):
        chip = place[2] ^ d
        token = pl.ds(pl.multiple_of(chip * TILE, TILE), TILE)
        for h in range(heads):
            u = insides[h][token, :] + dot(lefts[h][token, :], states[h])
            normed = u * lax.rsqrt(jnp.mean(u * u, axis=1, keepdims=True) + 1e-06)
            out[:, h * DH : (h + 1) * DH] = normed.astype(BF16)


def near_kernel(place, *refs):
    refs, (mine, theirs, rows) = refs[:-3], refs[-3:]
    pieces, weights = refs[: len(refs) // 2], refs[len(refs) // 2 :]

    @pl.when(pl.program_id(0) == 0)
    def _():
        for d, piece in enumerate(pieces):
            for side in range(2):
                where = pl.multiple_of((place[3] ^ side) * CHUNK, CHUNK)
                rows[d, side * CHUNK : (side + 1) * CHUNK, :] = piece[pl.ds(where, CHUNK), :]

    total = dot(rows[0], weights[0][...])
    for d in range(1, len(pieces)):
        total = total + dot(rows[d], weights[d][...])
    mine[...] = total[:CHUNK]
    theirs[...] = total[CHUNK:]


def far_kernel(side, place, piece, first, second, near, out):
    weight = jnp.concatenate([first[...], second[...]], axis=0)
    where = pl.multiple_of((place[3] ^ side) * CHUNK, CHUNK)
    total = near[...] + dot(piece[pl.ds(where, CHUNK), :], weight)
    out[...] = total.astype(out.dtype)


ANY = pl.BlockSpec(memory_space=pl.ANY)
HBM = pl.BlockSpec(memory_space=pltpu.HBM)


def small(kernel, shapes, *operands, specs=None, outs=None, scratch=(), flops=0, mib=24):
    return pl.pallas_call(
        kernel,
        out_shape=shapes,
        in_specs=specs or [SMEM if o.dtype == jnp.int32 else VMEM for o in operands],
        out_specs=outs or jax.tree.map(lambda _: VMEM, shapes),
        scratch_shapes=list(scratch),
        compiler_params=params(mib),
        cost_estimate=pl.CostEstimate(flops=flops, bytes_accessed=1 << 20, transcendentals=0),
    )(*operands)


def shards(activations, qkv_weight, level_proj, log_gate, prior_parts, out_weight):
    block, width = activations.shape
    heads = log_gate.shape[1]
    nz = lax.axis_size("ctx") // NX
    nh = lax.axis_size("head")
    ny = nh // 2
    z_bits = nz.bit_length() - 1
    chunks = block // CHUNK
    rows = heads * DH
    quarter = rows // NX
    shape = jax.ShapeDtypeStruct
    ctx = lax.axis_index("ctx").astype(jnp.int32)
    head = lax.axis_index("head").astype(jnp.int32)
    place = jnp.stack([ctx % NX, ctx // NX, head // 2, head % 2])

    def along_x(array, d):
        return lax.ppermute(
            array, "ctx", [(z * NX + x, z * NX + (x ^ d)) for z in range(nz) for x in range(NX)]
        )

    def across_z(array, target):
        return lax.ppermute(
            array, "ctx", [(z * NX + x, target(z) % nz * NX + x) for z in range(nz) for x in range(NX)]
        )

    def along_y(array, d):
        return lax.ppermute(
            array, "head", [(y * 2 + c, (y ^ d) * 2 + c) for y in range(ny) for c in range(2)]
        )

    below, above = along_y(out_weight, 1), along_y(out_weight, 3)
    gate = log_gate.T
    sent = shape((rows + TAIL + rows, DH), BF16)
    dma = pltpu.SemaphoreType.DMA
    kv, query_weight = small(
        keys_kernel,
        [shape((block, 2 * rows), BF16), shape((width, rows), BF16)],
        activations,
        qkv_weight,
        specs=[HBM] * 2,
        scratch=[
            pltpu.VMEM(activations.shape, BF16),
            pltpu.VMEM(qkv_weight.shape, BF16),
            dma((8,)),
            dma((8,)),
        ],
        flops=4 * block * width * rows,
        mib=50,
    )
    chunk_states, *payloads = small(
        states_kernel,
        [shape((chunks, heads, DH, DH), F32)] + [sent] * NX,
        place,
        kv,
        gate,
        prior_parts[0],
    )
    pieces = [payloads[0]] + [along_x(payloads[d], d) for d in range(1, NX)]

    query, level = small(
        level_kernel,
        [shape((block, rows), BF16), shape((block, DH), F32)],
        activations,
        query_weight,
        level_proj.T,
        payloads[0],
        specs=[VMEM] * 3 + [ANY],
        flops=4 * block * width * rows,
        mib=24,
    )

    def scaled(h, after):
        return small(
            functools.partial(scale_kernel, h),
            shape((block, (z_bits + PRIOR) * DH), BF16),
            query,
            level,
            gate,
            after,
            specs=[VMEM] * 3 + [ANY],
            flops=1 << 30,
        )

    lefts = [scaled(0, payloads[0])]
    low_states, onward, carry = small(
        within_kernel,
        [
            shape((2, heads, DH, DH), BF16),
            shape((quarter + TAIL + rows, DH), BF16),
            shape((8, DH), F32),
        ],
        place,
        pieces[0],
        pieces[2],
        pieces[3],
        pieces[1],
        lefts[0],
        specs=[SMEM] + [VMEM] * NX + [ANY],
    )

    def attend(h, after):
        return small(
            functools.partial(attend_kernel, h),
            shape((block, DH), F32),
            query,
            kv,
            level,
            gate,
            chunk_states,
            low_states,
            after,
            specs=[VMEM] * 6 + [ANY],
            flops=1 << 30,
        )

    got = across_z(onward, lambda z: z ^ 1)
    insides = [attend(0, onward)]
    state, onward, carry = small(
        pair_kernel,
        [shape((quarter, DH), BF16), shape(onward.shape, BF16), shape((8, DH), F32)],
        place,
        onward,
        got,
        carry,
        insides[0],
        specs=[SMEM] + [VMEM] * 3 + [ANY],
    )
    far = across_z(onward, lambda z: z + 3 if z % 2 else z - 3)
    skip = across_z(onward, lambda z: z + 2 if z % 2 else z - 2)
    near = across_z(onward, lambda z: z + 1 if z % 2 else z - 1)
    insides.append(attend(1, onward))
    halves = small(
        halves_kernel,
        [shape((rows // 2, width), BF16)] * 2,
        below,
        above,
        insides[1],
        specs=[ANY] * 3,
        outs=[VMEM] * 2,
        scratch=[dma((2,))],
        mib=4,
    )
    far_weight = along_y(halves[0], 3), along_y(halves[1], 1)
    payload, carry = small(
        pairs_kernel,
        [shape((z_bits * quarter + rows, DH), BF16), shape((8, DH), F32)],
        place,
        onward,
        far,
        skip,
        near,
        carry,
        state,
        halves[0],
        specs=[SMEM] + [VMEM] * 6 + [ANY],
    )
    lefts.append(scaled(1, payload))
    pieces = [payload] + [along_x(payload, d) for d in range(1, NX)]
    rows_out = shape((block // ny, rows), BF16)
    normed = [None] * ny
    normed[1], normed[3], normed[2], states = small(
        finish_kernel,
        [rows_out] * 3 + [shape((heads, (z_bits + PRIOR) * DH, DH), BF16)],
        place,
        carry,
        *insides,
        *lefts,
        pieces[0],
        pieces[1],
        pieces[2],
        pieces[3],
        flops=1 << 28,
    )
    normed[0] = small(
        functools.partial(rows_kernel, (0,)),
        rows_out,
        place,
        *insides,
        *lefts,
        states,
        normed[1],
        specs=[SMEM] + [VMEM] * 5 + [ANY],
        flops=1 << 28,
    )
    normed = [normed[0]] + [along_y(normed[d], d) for d in range(1, ny)]
    columns = 1024 if width % 1024 == 0 else width
    fixed = pl.BlockSpec((2 * CHUNK, rows), lambda i: (0, 0))
    weight_block = pl.BlockSpec((rows, columns), lambda i: (0, i))
    out_block = pl.BlockSpec((CHUNK, columns), lambda i: (0, i))
    half_block = pl.BlockSpec((rows // 2, columns), lambda i: (0, i))
    mine, theirs = pl.pallas_call(
        near_kernel,
        grid=(width // columns,),
        in_specs=[SMEM] + [fixed] * 3 + [weight_block] * 3,
        out_specs=[out_block] * 2,
        out_shape=[shape((CHUNK, width), F32)] * 2,
        scratch_shapes=[pltpu.VMEM((3, 2 * CHUNK, rows), BF16)],
        compiler_params=params(24),
        cost_estimate=pl.CostEstimate(flops=8 << 28, bytes_accessed=5 << 20, transcendentals=0),
    )(place, normed[0], normed[3], normed[1], out_weight, above, below)

    def add_far(side, near, dtype):
        return pl.pallas_call(
            functools.partial(far_kernel, side),
            grid=(width // columns,),
            in_specs=[SMEM, fixed, half_block, half_block, out_block],
            out_specs=out_block,
            out_shape=shape((CHUNK, width), dtype),
            compiler_params=params(24),
            cost_estimate=pl.CostEstimate(flops=1 << 28, bytes_accessed=3 << 20, transcendentals=0),
        )(place, normed[2], *far_weight, near)

    send = add_far(1, theirs, BF16)
    got = lax.ppermute(send, "head", [(i, i ^ 1) for i in range(nh)])
    keep = add_far(0, mine, F32)
    return (keep + got.astype(F32)).astype(BF16)


def solution(mesh):
    placed = (
        P("ctx", None),
        P(None, "head"),
        P(None, "head"),
        P("ctx", "head"),
        P("ctx", None, "head", None, None),
        P("head", None),
    )
    return jax.shard_map(
        shards, mesh=mesh, in_specs=placed, out_specs=P(("ctx", "head"), None), check_vma=False
    )
```
